128 devices in a mesh: seq: 8 (over x, core), expert: 16 (over y, z).
Axes of the slice: x: 4, y: 4, z: 4, core: 2. Of those that a mesh axis runs over, the one named last changes fastest.
Arguments:
- queries: bfloat16 [16, 1024, 4096], P('expert', 'seq'), may hold values from -6 to 6
- keys: bfloat16 [16, 1024, 512], P('expert', 'seq'), may hold values from -6 to 6
- values: bfloat16 [16, 1024, 512], P('expert', 'seq'), may hold values from -6 to 6
- w_out: bfloat16 [4096, 2048], P('seq'), may hold values from -0.09375 to 0.09375
- hidden_state: bfloat16 [16, 1024, 2048], P('expert', 'seq'), may hold values from -6 to 6
- norm_gain: bfloat16 [2048], replicated, may hold values from 0.099609375 to 1.8984375
- layer_grad: bfloat16 [16, 1024, 2048], P('expert', 'seq'), may hold values from -4 to 4
- hidden_grad: bfloat16 [16, 1024, 8, 768], P('expert', 'seq'), may hold values from -1.5 to 1.5
- routes: int32 [16, 1024, 8], P('expert', 'seq'), may hold values from 0 to 127, all different within a row; in each aligned block of 128 rows (0 to 127, 128 to 255, ..., all dimensions but the last counted through in order) at most 9 rows name the same one
- w_gate: bfloat16 [128, 2048, 768], P(('seq', 'expert')), may hold values from -0.125 to 0.125
- w_up: bfloat16 [128, 2048, 768], P(('seq', 'expert')), may hold values from -0.125 to 0.125
Outputs:
- query_grad: bfloat16 [16, 1024, 4096], P('expert', 'seq')
- key_grad: bfloat16 [16, 1024, 512], P('expert', 'seq')
- value_grad: bfloat16 [16, 1024, 512], P('expert', 'seq')
- residual_grad: bfloat16 [16, 1024, 2048], P('expert', 'seq')
- gate_grad: bfloat16 [128, 2048, 768], P(('seq', 'expert'))
- up_grad: bfloat16 [128, 2048, 768], P(('seq', 'expert'))
The draws below stay inside these ranges and needn't reach their ends.
Inputs may be any that keep to these rules, and one draw needn't show every extreme that they name: Among the 8 routes of each of the 128 tokens of one device, no expert is named more than 9 times, and a token names 8 different experts.
All inputs are finite; a program needn't handle non-finite values.
Results may differ from the reference program's by a relative error of at most 0.017.
Values may be sent and summed in bfloat16 or wider, within the bound.
A program may use at most 128 MiB of HBM per device.

```python
import math
import jax
import jax.numpy as jnp
import numpy as np
from jax import lax

D = 2048
QUERY_HEADS = 32
KEY_VALUE_HEADS = 4
HEAD_SIZE = 128
FFE = 768
TOP = 8
ATT_DEV = 128
EXPERTS = 128
SEQUENCE_LENGTH = 1024
SEQUENCE_COUNT = 16
CAP = 9
N_EXPERT = 16
DEVICES = 128


def draw_keys(key, part):
    key = jax.random.fold_in(key, 3)
    value_baseline = jnp.clip(jax.random.normal(key, (SEQUENCE_COUNT, SEQUENCE_LENGTH, KEY_VALUE_HEADS * HEAD_SIZE), jnp.float32), -6.0, 6.0)
    return value_baseline.astype(jnp.bfloat16)


def draw_queries(key, part):
    key = jax.random.fold_in(key, 5)
    value_baseline = jnp.clip(jax.random.normal(key, (SEQUENCE_COUNT, SEQUENCE_LENGTH, QUERY_HEADS * HEAD_SIZE), jnp.float32), -6.0, 6.0)
    return value_baseline.astype(jnp.bfloat16)


def block_scale(key, shape, cuts, least, top_value):
    factor_of, own = 1.0, jax.random.fold_in(key, 6)
    for dim, blocks in cuts:
        draws = jnp.exp(jax.random.uniform(jax.random.fold_in(own, dim), (blocks,), jnp.float32, least / len(cuts), top_value / len(cuts)))
        factor_of = factor_of * jnp.repeat(draws, shape[dim] // blocks).reshape([-1 if axis == dim else 1 for axis in range(len(shape))])
    return factor_of


def routed_block(key, own, number, rows, count, top, bound, skew):
    order = jax.random.permutation(key, count)
    packed, common = portions_of(count, rows * top, bound, skew, True), portions_of(count, rows * top, bound, skew, False)
    places = jnp.arange(count)

    def named(lengths, turn):
        used = int((lengths > 0).sum())
        fixed = max(1, used // 4)
        passed = fixed + (places - fixed + turn * (used - fixed)) % max(1, count - fixed)
        return jnp.zeros((count,), jnp.int32).at[order[jnp.where(places < fixed, places, passed)]].set(jnp.asarray(lengths, jnp.int32))

    lengths = jnp.where(number % 4 == 0, named(packed, number // 4), named(common, number - number // 4 - 1))
    mixed = jax.random.permutation(jax.random.fold_in(own, 3), count)
    source_of, receiver = mixed[0:count // 2 * 2:2], mixed[1:count // 2 * 2:2]
    margin = jnp.minimum(lengths[source_of] - 1, bound - lengths[receiver]) // 2
    margin = jnp.where((source_of == order[0]) | (receiver == order[0]) | (lengths[receiver] == 0), 0, jnp.maximum(margin, 0))
    passed = jax.random.randint(jax.random.fold_in(own, 4), (count // 2,), 0, 1 << 20) % (margin + 1)
    lengths = lengths.at[source_of].add(-passed).at[receiver].add(passed)
    items = jnp.searchsorted(jnp.cumsum(lengths), jnp.arange(rows * top), side="right").astype(jnp.int32)
    listing = items.reshape(top, rows).T
    listing = listing[jax.random.permutation(jax.random.fold_in(own, 1), rows)]
    turn = jax.random.randint(jax.random.fold_in(own, 2), (rows, 1), 0, top)
    return jnp.take_along_axis(listing, (jnp.arange(top)[None, :] + turn) % top, axis=1)


def portions_of(count, total, bound, lean, full):
    loads = [(1 << 20) // math.isqrt(standing ** lean) + 1 for standing in range(1, count + 1)]
    largest = bound if full else min(bound, max(-(-total // count), total * loads[0] // sum(loads)))
    least = 1 if total - largest >= count - 1 else 0
    holding, spare = [largest] + [least] * (count - 1), total - largest - least * (count - 1)
    while spare > 0:
        candidates = [i for i in range(1, count) if holding[i] < largest] or [i for i in range(1, count) if holding[i] < bound]
        whole, left = sum([loads[i] for i in candidates]), spare
        for i in candidates:
            addition = min(bound - holding[i], max(1, left * loads[i] // whole), spare)
            holding[i] = holding[i] + addition
            spare = spare - addition
    return np.array(holding)


def centred(key, extent, spread, reach, split=(), held_as=jnp.bfloat16):
    entries = spread * jax.random.normal(key, extent, jnp.float32)
    if split:
        entries = entries * block_scale(key, extent, split, -0.22, 0.18)
    return jnp.clip(entries, -reach, reach).astype(held_as)


def setup_inputs(seed: int = 0) -> dict:
    streams_of = jax.random.split(jax.random.key(seed), 12)
    queries = draw_queries(jax.random.fold_in(streams_of[11], 71), 0)
    keys = draw_keys(jax.random.fold_in(streams_of[11], 71), 0)
    values = centred(streams_of[2], (SEQUENCE_COUNT, SEQUENCE_LENGTH, KEY_VALUE_HEADS * HEAD_SIZE), 1.0, 6.0, ((0, 16), (1, 8)))
    w_out = centred(streams_of[3], (QUERY_HEADS * HEAD_SIZE, D), (QUERY_HEADS * HEAD_SIZE) ** -0.5, 0.09375, ((0, 8),))
    hidden_state = centred(streams_of[4], (SEQUENCE_COUNT, SEQUENCE_LENGTH, D), 1.0, 6.0, ((0, 16), (1, 8)))
    norm_gain = jnp.clip(1.0 + 0.18 * jax.random.normal(streams_of[5], (D,), jnp.float32), 0.099609375, 1.8984375).astype(jnp.bfloat16)
    layer_grad = centred(streams_of[6], (SEQUENCE_COUNT, SEQUENCE_LENGTH, D), 0.5, 4.0, ((0, 16), (1, 8)))
    hidden_grad = centred(streams_of[7], (SEQUENCE_COUNT, SEQUENCE_LENGTH, TOP, FFE), 0.25, 1.5, ((0, 16), (1, 8)))
    routes_keys = jax.random.split(jax.random.fold_in(streams_of[8], 1), SEQUENCE_COUNT * SEQUENCE_LENGTH // ATT_DEV)
    routes_turns = jax.random.permutation(jax.random.fold_in(streams_of[8], 3), SEQUENCE_COUNT * SEQUENCE_LENGTH // ATT_DEV)
    routes = jax.vmap(lambda own, number: routed_block(jax.random.fold_in(streams_of[8], 2), own, number, ATT_DEV, EXPERTS, TOP, CAP, 1))(routes_keys, routes_turns).reshape((SEQUENCE_COUNT, SEQUENCE_LENGTH, TOP))
    w_gate = centred(streams_of[9], (EXPERTS, D, FFE), D ** -0.5, 0.125, ((0, 128),))
    w_up = centred(streams_of[10], (EXPERTS, D, FFE), D ** -0.5, 0.125, ((0, 128),))
    return {"queries": queries, "keys": keys, "values": values, "w_out": w_out, "hidden_state": hidden_state, "norm_gain": norm_gain, "layer_grad": layer_grad, "hidden_grad": hidden_grad, "routes": routes, "w_gate": w_gate, "w_up": w_up}


def attend(query_rows, key_rows, value_rows, grad_rows, query_pos, key_pos):
    factor = query_rows.shape[-1] ** (-0.5)
    scores = jnp.einsum('ikrd,jkd->krij', query_rows, key_rows, preferred_element_type=jnp.float32) * factor
    allowed = key_pos[None, :] <= query_pos[:, None]
    scores = jnp.where(allowed, scores, -1e+30)
    highest = lax.optimization_barrier(jnp.max(scores, axis=-1, keepdims=True))
    exp_scores = jnp.exp(scores - highest)
    probs_full = exp_scores / lax.optimization_barrier(jnp.sum(exp_scores, axis=-1, keepdims=True))
    probs_low = probs_full.astype(jnp.bfloat16)
    value_grad = jnp.einsum('krij,ikrd->jkd', probs_low, grad_rows, preferred_element_type=jnp.float32)
    prob_grad = jnp.einsum('ikrd,jkd->krij', grad_rows, value_rows, preferred_element_type=jnp.float32)
    delta_sum = lax.optimization_barrier(jnp.sum(probs_full * prob_grad, axis=-1, keepdims=True))
    score_grad = (probs_full * (prob_grad - delta_sum)).astype(jnp.bfloat16)
    query_grad = (jnp.einsum('krij,jkd->ikrd', score_grad, key_rows, preferred_element_type=jnp.float32) * factor).astype(jnp.bfloat16)
    key_grad = jnp.einsum('krij,ikrd->jkd', score_grad, query_rows, preferred_element_type=jnp.float32) * factor
    return (query_grad, key_grad, value_grad)

def expert_rows(rows_in, rows_grad, gate_weight, up_weight):
    gate_pre = jnp.dot(rows_in, gate_weight, preferred_element_type=jnp.float32)
    up_pre = jnp.dot(rows_in, up_weight, preferred_element_type=jnp.float32)
    sig_gate = jax.nn.sigmoid(gate_pre)
    gate_part = (rows_grad * up_pre * sig_gate * (1.0 + gate_pre * (1.0 - sig_gate))).astype(jnp.bfloat16)
    up_part = (rows_grad * gate_pre * sig_gate).astype(jnp.bfloat16)
    rows_back = (jnp.dot(gate_part, gate_weight.T, preferred_element_type=jnp.float32) + jnp.dot(up_part, up_weight.T, preferred_element_type=jnp.float32)).astype(jnp.bfloat16)
    gate_sum = lax.dot_general(rows_in, gate_part, (((0,), (0,)), ((), ())), preferred_element_type=jnp.float32)
    up_sum = lax.dot_general(rows_in, up_part, (((0,), (0,)), ((), ())), preferred_element_type=jnp.float32)
    return (rows_back, gate_sum.astype(jnp.bfloat16), up_sum.astype(jnp.bfloat16))

def reference(queries, keys, values, w_out, hidden_state, norm_gain, layer_grad, hidden_grad, routes, w_gate, w_up):
    state_full = hidden_state.astype(jnp.float32)
    rstd = lax.rsqrt(lax.optimization_barrier(jnp.mean(state_full * state_full, axis=-1, keepdims=True)) + 1e-06)
    normed = state_full * rstd
    gain_full = norm_gain.astype(jnp.float32)
    expert_in = (normed * gain_full).astype(jnp.bfloat16)
    route_flat = routes.reshape(-1).astype(jnp.int32)
    route_count = route_flat.shape[0]
    one_hot = (route_flat[:, None] == jnp.arange(EXPERTS, dtype=jnp.int32)[None, :]).astype(jnp.int32)
    blocked = one_hot.reshape(route_count // (ATT_DEV * TOP), ATT_DEV * TOP, EXPERTS)
    earlier = jnp.cumsum(blocked, axis=1) - blocked
    rank_in_block = lax.optimization_barrier(jnp.sum(earlier * blocked, axis=2)).reshape(-1).astype(jnp.int32)
    token_index = jnp.arange(route_count, dtype=jnp.int32) // TOP
    sequence_index = token_index // SEQUENCE_LENGTH
    source = token_index % SEQUENCE_LENGTH // ATT_DEV * N_EXPERT + sequence_index
    slot_index = source * CAP + rank_in_block
    table = jnp.full((EXPERTS, DEVICES * CAP), route_count, jnp.int32)
    table = table.at[route_flat, slot_index].set(jnp.arange(route_count, dtype=jnp.int32))
    input_pad = jnp.concatenate([expert_in.reshape(-1, D), jnp.zeros((1, D), jnp.bfloat16)], axis=0)
    grad_pad = jnp.concatenate([hidden_grad.reshape(-1, FFE), jnp.zeros((1, FFE), hidden_grad.dtype)], axis=0)

    def one_expert(accum, inputs):
        slots, gate_weight, up_weight = inputs
        token_rows = (slots // TOP).astype(jnp.int32)
        rows_back, gate_sum, up_sum = expert_rows(input_pad[token_rows], grad_pad[slots], gate_weight, up_weight)
        accum = accum.at[token_rows].add(rows_back.astype(jnp.float32))
        return (accum, (gate_sum, up_sum))
    accum, (gate_grad, up_grad) = lax.scan(one_expert, jnp.zeros((SEQUENCE_COUNT * SEQUENCE_LENGTH + 1, D), jnp.float32), (table, w_gate, w_up))
    routed_grad = accum[:SEQUENCE_COUNT * SEQUENCE_LENGTH].reshape(SEQUENCE_COUNT, SEQUENCE_LENGTH, D)
    weighted = gain_full * routed_grad
    inner = lax.optimization_barrier(jnp.mean(weighted * normed, axis=-1, keepdims=True))
    residual_grad = (layer_grad.astype(jnp.float32) + rstd * (weighted - normed * inner)).astype(jnp.bfloat16)

    def project(rows):
        return jnp.dot(rows, w_out.T, preferred_element_type=jnp.float32).astype(jnp.bfloat16)
    out_grad = lax.map(project, residual_grad)
    positions = jnp.arange(SEQUENCE_LENGTH, dtype=jnp.int32)
    group_width = QUERY_HEADS // KEY_VALUE_HEADS

    def one_head(inputs):
        query_head, key_head, value_head, grad_head = inputs
        return attend(query_head, key_head, value_head, grad_head, positions, positions)

    def one_sequence(inputs):
        query_sequence, key_sequence, value_sequence, gradient_sequence = inputs
        query_head_rows = jnp.moveaxis(query_sequence.reshape(SEQUENCE_LENGTH, KEY_VALUE_HEADS, group_width, HEAD_SIZE), 1, 0)[:, :, None]
        gradient_heads = jnp.moveaxis(gradient_sequence.reshape(SEQUENCE_LENGTH, KEY_VALUE_HEADS, group_width, HEAD_SIZE), 1, 0)[:, :, None]
        key_head_rows = jnp.moveaxis(key_sequence.reshape(SEQUENCE_LENGTH, KEY_VALUE_HEADS, HEAD_SIZE), 1, 0)[:, :, None]
        value_head_rows = jnp.moveaxis(value_sequence.reshape(SEQUENCE_LENGTH, KEY_VALUE_HEADS, HEAD_SIZE), 1, 0)[:, :, None]
        query_part, key_portion, value_portion = lax.map(one_head, (query_head_rows, key_head_rows, value_head_rows, gradient_heads))
        return (jnp.moveaxis(query_part[:, :, 0], 0, 1).reshape(SEQUENCE_LENGTH, QUERY_HEADS * HEAD_SIZE), jnp.moveaxis(key_portion[:, :, 0], 0, 1).astype(jnp.bfloat16).reshape(SEQUENCE_LENGTH, KEY_VALUE_HEADS * HEAD_SIZE), jnp.moveaxis(value_portion[:, :, 0], 0, 1).astype(jnp.bfloat16).reshape(SEQUENCE_LENGTH, KEY_VALUE_HEADS * HEAD_SIZE))
    query_grad, key_grad, value_grad = lax.map(one_sequence, (queries, keys, values, out_grad))
    return (query_grad, key_grad, value_grad, residual_grad, gate_grad, up_grad)
```

```python
import functools

import jax
import jax.numpy as jnp
from jax import lax
from jax.experimental import pallas as pl
from jax.experimental.pallas import tpu as pltpu
from jax.sharding import PartitionSpec as P

D = 2048
QUERY_HEADS = 32
KEY_VALUE_HEADS = 4
HEAD_SIZE = 128
FFE = 768
TOP = 8
LOG2E = 1.4426950408889634

NN = (((1,), (0,)), ((), ()))
NT = (((1,), (1,)), ((), ()))
TN = (((0,), (0,)), ((), ()))


def dot(a, b, dims):
    return lax.dot_general(a, b, dims, preferred_element_type=jnp.float32)


def attention_kernel(heads, block, qkv_ref, res_ref, w_ref, out_ref, grad, key_t, dk, dv):
    length = qkv_ref.shape[0]
    width = heads * HEAD_SIZE
    factor = HEAD_SIZE ** (-0.5)
    for lower in range(0, length, block):
        rows = pl.ds(lower, block)
        grad[rows, :] = dot(res_ref[rows, :], w_ref[...], NT).astype(jnp.bfloat16)
    key_t[...] = qkv_ref[:, width : width + HEAD_SIZE].astype(jnp.float32).T.astype(jnp.bfloat16)
    dk[...] = jnp.zeros_like(dk)
    dv[...] = jnp.zeros_like(dv)
    for lower in range(0, length, block):
        rows, upper = pl.ds(lower, block), lower + block
        key_pos = lax.broadcasted_iota(jnp.int32, (block, block), 0)
        query_pos = lax.broadcasted_iota(jnp.int32, (block, block), 1)
        for head in range(heads):
            columns = pl.ds(head * HEAD_SIZE, HEAD_SIZE)
            query, out_grad = qkv_ref[rows, columns], grad[rows, columns]
            keys = qkv_ref[0:upper, width : width + HEAD_SIZE]
            values = qkv_ref[0:upper, width + HEAD_SIZE : width + 2 * HEAD_SIZE]
            scores = dot(keys, query, NT) * (factor * LOG2E)
            last = jnp.where(key_pos <= query_pos, scores[lower:upper], -1e30)
            scores = last if lower == 0 else jnp.concatenate([scores[:lower], last], axis=0)
            exps = jnp.exp2(scores - jnp.max(scores, axis=0, keepdims=True))
            probs = exps * (1.0 / jnp.sum(exps, axis=0, keepdims=True))
            dv[0:upper, :] += dot(probs.astype(jnp.bfloat16), out_grad, NN)
            prob_grad = dot(values, out_grad, NT)
            delta = jnp.sum(probs * prob_grad, axis=0, keepdims=True)
            score_grad = (probs * (prob_grad - delta)).astype(jnp.bfloat16)
            dk[0:upper, :] += dot(score_grad, query, NN)
            query_grad = dot(key_t[:, 0:upper], score_grad, NN) * factor
            out_ref[rows, columns] = query_grad.T.astype(jnp.bfloat16)
    out_ref[:, width : width + HEAD_SIZE] = (dk[...] * factor).astype(jnp.bfloat16)
    out_ref[:, width + HEAD_SIZE : width + 2 * HEAD_SIZE] = dv[...].astype(jnp.bfloat16)


def attention_core(qkv, residual, w_out):
    length, heads = qkv.shape[0], w_out.shape[0] // HEAD_SIZE
    return pl.pallas_call(
        functools.partial(attention_kernel, heads, min(256, length)),
        out_shape=jax.ShapeDtypeStruct(qkv.shape, jnp.bfloat16),
        in_specs=[pl.BlockSpec(memory_space=pltpu.VMEM)] * 3,
        out_specs=pl.BlockSpec(memory_space=pltpu.VMEM),
        scratch_shapes=[
            pltpu.VMEM((length, heads * HEAD_SIZE), jnp.bfloat16),
            pltpu.VMEM((HEAD_SIZE, length), jnp.bfloat16),
            pltpu.VMEM((length, HEAD_SIZE), jnp.float32),
            pltpu.VMEM((length, HEAD_SIZE), jnp.float32),
        ],
        compiler_params=pltpu.CompilerParams(vmem_limit_bytes=48 << 20),
        cost_estimate=pl.CostEstimate(
            flops=9_000_000_000, bytes_accessed=10_000_000, transcendentals=3_000_000
        ),
        name="attention_core",
    )(qkv, residual, w_out)


def exchange_heads(queries, keys, values):
    group = lax.axis_size("seq")
    tokens = queries.shape[1]
    repeat = group // KEY_VALUE_HEADS
    query_send = jnp.transpose(queries[0].reshape(tokens, group, -1), (1, 0, 2))

    def spread(array):
        by_head = jnp.transpose(array[0].reshape(tokens, KEY_VALUE_HEADS, HEAD_SIZE), (1, 0, 2))
        return jnp.repeat(by_head, repeat, axis=0)

    send = jnp.concatenate([query_send, spread(keys), spread(values)], axis=-1)
    got = lax.all_to_all(send, "seq", split_axis=0, concat_axis=0, tiled=True)
    return got.reshape(group * tokens, -1)


def return_heads(grads):
    group = lax.axis_size("seq")
    tokens = grads.shape[0] // group
    width = grads.shape[1] - 2 * HEAD_SIZE
    got = lax.all_to_all(
        grads.reshape(group, tokens, -1), "seq", split_axis=0, concat_axis=0, tiled=True
    )
    query_out = jnp.transpose(got[:, :, :width], (1, 0, 2)).reshape(1, tokens, group * width)

    def total(part):
        part = part.astype(jnp.float32).reshape(KEY_VALUE_HEADS, -1, tokens, HEAD_SIZE)
        part = jnp.sum(part, axis=1).astype(jnp.bfloat16)
        return jnp.transpose(part, (1, 0, 2)).reshape(1, tokens, KEY_VALUE_HEADS * HEAD_SIZE)

    return (
        query_out,
        total(got[:, :, width : width + HEAD_SIZE]),
        total(got[:, :, width + HEAD_SIZE :]),
    )


def expert_rows(rows_in, rows_grad, gate_weight, up_weight):
    gate_pre = dot(rows_in, gate_weight, NN)
    up_pre = dot(rows_in, up_weight, NN)
    sig_gate = jax.nn.sigmoid(gate_pre)
    gate_part = (rows_grad * up_pre * sig_gate * (1.0 + gate_pre * (1.0 - sig_gate))).astype(
        jnp.bfloat16
    )
    up_part = (rows_grad * gate_pre * sig_gate).astype(jnp.bfloat16)
    rows_back = (dot(gate_part, gate_weight, NT) + dot(up_part, up_weight, NT)).astype(jnp.bfloat16)
    gate_sum = dot(rows_in, gate_part, TN)
    up_sum = dot(rows_in, up_part, TN)
    return (rows_back, gate_sum.astype(jnp.bfloat16), up_sum.astype(jnp.bfloat16))


def routed_grads(expert_in, hidden_grad, routes, w_gate, w_up):
    devices = lax.axis_size(("seq", "expert"))
    tokens = expert_in.shape[0]
    route = routes[0]
    named = route[:, :, None] == jnp.arange(devices, dtype=jnp.int32)
    count = jnp.sum(named.astype(jnp.bfloat16), axis=1)
    earlier = (jnp.arange(tokens)[:, None] > jnp.arange(tokens)[None, :]).astype(jnp.bfloat16)
    rank = dot(earlier, count, NN)
    route_rank = jnp.sum(jnp.where(named, rank[:, None, :], 0.0), axis=2).astype(jnp.int32)
    slots = jnp.arange(8, dtype=jnp.float32)
    rank_t = jnp.where(count > 0, rank, -1.0).T
    token_main = (rank_t[:, None, :] == slots[None, :, None]).astype(jnp.bfloat16)
    token_main = token_main.reshape(devices * 8, tokens)
    token_last = (rank_t == 8.0).astype(jnp.bfloat16)
    place_main = jnp.where(route_rank < 8, route * 8 + route_rank, -1).reshape(1, -1)
    place_last = jnp.where(route_rank == 8, route, -1).reshape(1, -1)
    route_main = (place_main == jnp.arange(devices * 8, dtype=jnp.int32)[:, None]).astype(
        jnp.bfloat16
    )
    route_last = (place_last == jnp.arange(devices, dtype=jnp.int32)[:, None]).astype(jnp.bfloat16)
    grads = hidden_grad[0].reshape(tokens * TOP, FFE)
    send_main = jnp.concatenate(
        [
            dot(token_main, expert_in, NN).astype(jnp.bfloat16),
            dot(route_main, grads, NN).astype(jnp.bfloat16),
        ],
        axis=1,
    )
    last_in = dot(token_last, expert_in, NN).astype(jnp.bfloat16)
    last_grad = dot(route_last, grads, NN).astype(jnp.bfloat16)
    last_grad = jnp.pad(last_grad.reshape(devices, 6, 128), ((0, 0), (0, 2), (0, 0)))
    send = jnp.concatenate(
        [
            send_main.reshape(devices, 8, D + FFE),
            last_in.reshape(devices, 8, D // 8),
            last_grad,
        ],
        axis=2,
    )
    got = lax.all_to_all(send, ("seq", "expert"), split_axis=0, concat_axis=0, tiled=True)
    rows_in = jnp.concatenate(
        [
            got[:, :, :D].reshape(devices * 8, D),
            got[:, :, D + FFE : D + FFE + D // 8].reshape(devices, D),
        ],
        axis=0,
    )
    rows_grad = jnp.concatenate(
        [
            got[:, :, D : D + FFE].reshape(devices * 8, FFE),
            got[:, :6, D + FFE + D // 8 :].reshape(devices, FFE),
        ],
        axis=0,
    )
    rows_back, gate_sum, up_sum = expert_rows(rows_in, rows_grad, w_gate[0], w_up[0])
    back_send = jnp.concatenate(
        [
            rows_back[: devices * 8].reshape(devices, 8, D),
            rows_back[devices * 8 :].reshape(devices, 8, D // 8),
        ],
        axis=2,
    )
    back = lax.all_to_all(back_send, ("seq", "expert"), split_axis=0, concat_axis=0, tiled=True)
    routed_grad = dot(token_main, back[:, :, :D].reshape(devices * 8, D), TN)
    routed_grad += dot(token_last, back[:, :, D:].reshape(devices, D), TN)
    return (routed_grad, gate_sum[None], up_sum[None])


def local(
    queries,
    keys,
    values,
    w_out,
    hidden_state,
    norm_gain,
    layer_grad,
    hidden_grad,
    routes,
    w_gate,
    w_up,
):
    state_full = hidden_state[0].astype(jnp.float32)
    rstd = lax.rsqrt(jnp.mean(state_full * state_full, axis=-1, keepdims=True) + 1e-06)
    normed = state_full * rstd
    gain_full = norm_gain.astype(jnp.float32)
    expert_in = (normed * gain_full).astype(jnp.bfloat16)
    routed_grad, gate_grad, up_grad = routed_grads(expert_in, hidden_grad, routes, w_gate, w_up)
    qkv = exchange_heads(queries, keys, values)
    weighted = gain_full * routed_grad
    inner = jnp.mean(weighted * normed, axis=-1, keepdims=True)
    residual_rows = (layer_grad[0].astype(jnp.float32) + rstd * (weighted - normed * inner)).astype(
        jnp.bfloat16
    )
    residual_all = lax.all_gather(residual_rows, "seq", axis=0, tiled=True)
    grads = attention_core(qkv, residual_all, w_out)
    query_out, key_out, value_out = return_heads(grads)
    return (query_out, key_out, value_out, residual_rows[None], gate_grad, up_grad)


def solution(mesh):
    return jax.shard_map(
        local,
        mesh=mesh,
        in_specs=(
            P("expert", "seq", None),
            P("expert", "seq", None),
            P("expert", "seq", None),
            P("seq", None),
            P("expert", "seq", None),
            P(),
            P("expert", "seq", None),
            P("expert", "seq", None, None),
            P("expert", "seq", None),
            P(("seq", "expert"), None, None),
            P(("seq", "expert"), None, None),
        ),
        out_specs=(
            P("expert", "seq", None),
            P("expert", "seq", None),
            P("expert", "seq", None),
            P("expert", "seq", None),
            P(("seq", "expert"), None, None),
            P(("seq", "expert"), None, None),
        ),
        check_vma=False,
    )
```

```python
import functools

import jax
import jax.numpy as jnp
from jax import lax
from jax.experimental import pallas as pl
from jax.experimental.pallas import tpu as pltpu
from jax.sharding import PartitionSpec as P

D = 2048
QUERY_HEADS = 32
KEY_VALUE_HEADS = 4
HEAD_SIZE = 128
FFE = 768
TOP = 8
LOG2E = 1.4426950408889634

NN = (((1,), (0,)), ((), ()))
NT = (((1,), (1,)), ((), ()))
TN = (((0,), (0,)), ((), ()))
MESH = pl.DeviceIdType.MESH


def dot(a, b, dims):
    return lax.dot_general(a, b, dims, preferred_element_type=jnp.float32)


def attention_kernel(heads, block, qkv_ref, res_ref, w_ref, out_ref, grad, key_t, dk, dv):
    length = qkv_ref.shape[0]
    width = heads * HEAD_SIZE
    factor = HEAD_SIZE ** (-0.5)
    for lower in range(0, length, block):
        rows = pl.ds(lower, block)
        grad[rows, :] = dot(res_ref[rows, :], w_ref[...], NT).astype(jnp.bfloat16)
    key_t[...] = qkv_ref[:, width : width + HEAD_SIZE].astype(jnp.float32).T.astype(jnp.bfloat16)
    dk[...] = jnp.zeros_like(dk)
    dv[...] = jnp.zeros_like(dv)
    for lower in range(0, length, block):
        rows, upper = pl.ds(lower, block), lower + block
        key_pos = lax.broadcasted_iota(jnp.int32, (block, block), 0)
        query_pos = lax.broadcasted_iota(jnp.int32, (block, block), 1)
        for head in range(heads):
            columns = pl.ds(head * HEAD_SIZE, HEAD_SIZE)
            query, out_grad = qkv_ref[rows, columns], grad[rows, columns]
            keys = qkv_ref[0:upper, width : width + HEAD_SIZE]
            values = qkv_ref[0:upper, width + HEAD_SIZE : width + 2 * HEAD_SIZE]
            scores = dot(keys, query, NT) * (factor * LOG2E)
            last = jnp.where(key_pos <= query_pos, scores[lower:upper], -1e30)
            scores = last if lower == 0 else jnp.concatenate([scores[:lower], last], axis=0)
            exps = jnp.exp2(scores - jnp.max(scores, axis=0, keepdims=True))
            probs = exps * (1.0 / jnp.sum(exps, axis=0, keepdims=True))
            dv[0:upper, :] += dot(probs.astype(jnp.bfloat16), out_grad, NN)
            prob_grad = dot(values, out_grad, NT)
            delta = jnp.sum(probs * prob_grad, axis=0, keepdims=True)
            score_grad = (probs * (prob_grad - delta)).astype(jnp.bfloat16)
            dk[0:upper, :] += dot(score_grad, query, NN)
            query_grad = dot(key_t[:, 0:upper], score_grad, NN) * factor
            out_ref[rows, columns] = query_grad.T.astype(jnp.bfloat16)
    out_ref[:, width : width + HEAD_SIZE] = (dk[...] * factor).astype(jnp.bfloat16)
    out_ref[:, width + HEAD_SIZE : width + 2 * HEAD_SIZE] = dv[...].astype(jnp.bfloat16)


def attention_core(qkv, residual, w_out):
    length, heads = qkv.shape[0], w_out.shape[0] // HEAD_SIZE
    return pl.pallas_call(
        functools.partial(attention_kernel, heads, min(256, length)),
        out_shape=jax.ShapeDtypeStruct(qkv.shape, jnp.bfloat16),
        in_specs=[pl.BlockSpec(memory_space=pltpu.VMEM)] * 3,
        out_specs=pl.BlockSpec(memory_space=pltpu.VMEM),
        scratch_shapes=[
            pltpu.VMEM((length, heads * HEAD_SIZE), jnp.bfloat16),
            pltpu.VMEM((HEAD_SIZE, length), jnp.bfloat16),
            pltpu.VMEM((length, HEAD_SIZE), jnp.float32),
            pltpu.VMEM((length, HEAD_SIZE), jnp.float32),
        ],
        compiler_params=pltpu.CompilerParams(vmem_limit_bytes=48 << 20),
        cost_estimate=pl.CostEstimate(
            flops=9_000_000_000, bytes_accessed=10_000_000, transcendentals=3_000_000
        ),
        name="attention_core",
    )(qkv, residual, w_out)


def return_heads(grads):
    group = lax.axis_size("seq")
    tokens = grads.shape[0] // group
    width = grads.shape[1] - 2 * HEAD_SIZE
    got = lax.all_to_all(
        grads.reshape(group, tokens, -1), "seq", split_axis=0, concat_axis=0, tiled=True
    )
    query_out = jnp.transpose(got[:, :, :width], (1, 0, 2)).reshape(1, tokens, group * width)

    def total(part):
        part = part.astype(jnp.float32).reshape(KEY_VALUE_HEADS, -1, tokens, HEAD_SIZE)
        part = jnp.sum(part, axis=1).astype(jnp.bfloat16)
        return jnp.transpose(part, (1, 0, 2)).reshape(1, tokens, KEY_VALUE_HEADS * HEAD_SIZE)

    return (
        query_out,
        total(got[:, :, width : width + HEAD_SIZE]),
        total(got[:, :, width + HEAD_SIZE :]),
    )


ORDER = 37
GROUP = 32
GROUPS = 4
ROWS = GROUP * 8
PART = ROWS + GROUP
TAIL = D // 8
WIDE = D + FFE
MESSAGE = WIDE + TAIL + HEAD_SIZE


def place_of(order, sign, here):
    x, c, y, z = here
    code = lax.rem(order * ORDER, 128)
    dc, dx, dy, dz = lax.rem(code, 2), lax.rem(code // 2, 4), lax.rem(code // 8, 4), code // 32
    if sign < 0:
        dx, dy, dz = 4 - dx, 4 - dy, 4 - dz
    return (
        lax.rem(x + dx, 4) * 2 + lax.rem(c + dc, 2),
        lax.rem(y + dy, 4) * 4 + lax.rem(z + dz, 4),
    )


def expert_of(order, here):
    seq, expert = place_of(order, 1, here)
    return seq * 16 + expert


def expert_kernel(
    state_ref, gain_ref, layer_ref, grads_ref, routes_ref, gate_hbm, up_hbm, query_hbm, key_hbm,
    value_hbm, residual_ref, gate_out, up_out, query_all, key_all, value_all,
    send, recv, back, back_recv, weights, rows_in, parts, stage, expert_in, hot, hot_t, last,
    codes, last_rows, weight_sem, send_sem, recv_sem, back_sem, back_recv_sem, out_sem,
    head_send, head_recv,
):
    seq, expert = lax.axis_index("seq"), lax.axis_index("expert")
    here = (seq // 2, lax.rem(seq, 2), expert // 4, lax.rem(expert, 4))
    tokens = state_ref.shape[0]
    bf16, f32 = jnp.bfloat16, jnp.float32

    def iota(shape, axis):
        return lax.broadcasted_iota(jnp.int32, shape, axis)

    barrier = pltpu.get_barrier_semaphore()

    def greet(order, carry):
        pl.semaphore_signal(barrier, inc=1, device_id=place_of(order, 1, here), device_id_type=MESH)
        return carry

    lax.fori_loop(1, 128, greet, 0)
    gate_copy = pltpu.make_async_copy(gate_hbm, weights.at[:, pl.ds(0, FFE)], weight_sem.at[0])
    up_copy = pltpu.make_async_copy(up_hbm, weights.at[:, pl.ds(FFE, FFE)], weight_sem.at[1])
    gate_copy.start()
    up_copy.start()

    gain = gain_ref[...].astype(f32)
    state = state_ref[...].astype(f32)
    rstd = lax.rsqrt(jnp.mean(state * state, axis=-1, keepdims=True) + 1e-06)
    expert_in[...] = (state * rstd * gain).astype(bf16)

    lanes = iota((tokens, 128), 1)
    named = [routes_ref[:, k : k + 1] == lanes for k in range(TOP)]
    count = sum(jnp.where(n, 1.0, 0.0) for n in named)
    earlier = jnp.where(iota((tokens, tokens), 0) > iota((tokens, tokens), 1), 1.0, 0.0)
    rank = dot(earlier.astype(bf16), count.astype(bf16), NN)
    columns = iota((tokens, tokens * TOP), 1) - iota((tokens, tokens * TOP), 0) * TOP
    spread_codes = jnp.zeros((tokens, tokens * TOP), f32)
    for k in range(TOP):
        route_rank = jnp.sum(jnp.where(named[k], rank, 0.0), axis=1, keepdims=True)
        code = routes_ref[:, k : k + 1].astype(f32) * 16.0 + route_rank
        spread_codes = jnp.where(columns == k, code, spread_codes)
    codes[...] = jnp.sum(spread_codes, axis=0, keepdims=True)
    target = expert_of(iota((128, 128), 0), here)
    ordered = jnp.where(target == iota((128, 128), 1), 1.0, 0.0).astype(bf16)
    rank_t = dot(ordered, jnp.where(count > 0.0, rank, -1.0).astype(bf16), NT)
    slot = iota((128, 8, tokens), 1).astype(f32)
    rank_wide = jnp.broadcast_to(rank_t[:, None, :], (128, 8, tokens))
    hot_full = jnp.where(rank_wide == slot, 1.0, 0.0).reshape(1024, tokens)
    hot[...] = hot_full.astype(bf16)
    hot_t[:, 0:1024] = hot_full.T.astype(bf16)
    last_full = jnp.where(rank_wide == 8.0, 1.0, 0.0).reshape(1024, tokens)
    hot_t[:, 1024:2048] = last_full.T.astype(bf16)
    last[...] = jnp.where(rank_t == 8.0, 1.0, 0.0).astype(bf16)

    row, col = iota((ROWS, ROWS), 0), iota((ROWS, ROWS), 1)
    spread = jnp.where(col == lax.rem(row, 8) * GROUP + row // 8, 1.0, 0.0).astype(bf16)
    gather = jnp.where(row == lax.rem(col, 8) * GROUP + col // 8, 1.0, 0.0).astype(bf16)

    pl.semaphore_wait(barrier, 127)

    def head_copies(step):
        dx, dc = step // 2, lax.rem(step, 2)
        to = lax.rem(here[0] + dx, 4) * 2 + lax.rem(here[1] + dc, 2)
        rows = pl.ds(pl.multiple_of(seq * tokens, tokens), tokens)
        wide = pl.ds(pl.multiple_of(to * 512, 512), 512)
        narrow = pl.ds(pl.multiple_of(to // 2 * HEAD_SIZE, HEAD_SIZE), HEAD_SIZE)
        return to, (
            (query_hbm.at[:, wide], query_all.at[rows, :]),
            (key_hbm.at[:, narrow], key_all.at[rows, :]),
            (value_hbm.at[:, narrow], value_all.at[rows, :]),
        )

    def head_remote(step):
        to, pairs = head_copies(step)
        return [
            pltpu.make_async_remote_copy(
                src_ref=source, dst_ref=target_ref, send_sem=head_send.at[n, step],
                recv_sem=head_recv.at[n, step], device_id=(to, expert), device_id_type=MESH,
            )
            for n, (source, target_ref) in enumerate(pairs)
        ]

    own = [
        pltpu.make_async_copy(source, target_ref, head_send.at[n, 0])
        for n, (source, target_ref) in enumerate(head_copies(0)[1])
    ]
    for copy in own:
        copy.start()

    def send_heads(step, carry):
        for copy in head_remote(step):
            copy.start()
        return carry

    lax.fori_loop(1, 8, send_heads, 0)

    def dispatch(g, carry):
        at = pl.ds(g * GROUP, GROUP)
        rows = pl.ds(pl.multiple_of(g * ROWS, ROWS), ROWS)
        first = g * GROUP
        x_rows = dot(hot[rows, :], expert_in[...], NN).astype(bf16)
        send[at, :, 0:D] = x_rows.reshape(GROUP, 8, D)
        number = iota((ROWS, 128), 0)
        row_code = (expert_of(first + number // 8, here) * 16 + lax.rem(number, 8)).astype(f32)
        last_code = (expert_of(first + iota((GROUP, 128), 0), here) * 16 + 8).astype(f32)

        def one_hot(code):
            pieces = [
                jnp.where(codes[:, j * 128 : (j + 1) * 128] == code, 1.0, 0.0).astype(bf16)
                for j in range(TOP)
            ]
            return jnp.concatenate(pieces, axis=1)

        h_rows = dot(one_hot(row_code), grads_ref[...], NN).astype(bf16)
        send[at, :, D:WIDE] = h_rows.reshape(GROUP, 8, FFE)
        x_last = dot(last[pl.ds(pl.multiple_of(first, GROUP), GROUP), :], expert_in[...], NN)
        x_last = x_last.astype(bf16)
        h_last = dot(one_hot(last_code), grads_ref[...], NN).astype(bf16)
        x_stack = jnp.concatenate([x_last[:, s * TAIL : (s + 1) * TAIL] for s in range(8)], axis=0)
        h_stack = jnp.concatenate([h_last[:, s * 128 : (s + 1) * 128] for s in range(6)], axis=0)
        x_tail = dot(spread, x_stack, NN).astype(bf16)
        h_tail = dot(spread[:, 0 : 6 * GROUP], h_stack, NN).astype(bf16)
        send[at, :, WIDE : WIDE + TAIL] = x_tail.reshape(GROUP, 8, TAIL)
        send[at, :, WIDE + TAIL : MESSAGE] = h_tail.reshape(GROUP, 8, HEAD_SIZE)

        def start(order, inner):
            pltpu.make_async_remote_copy(
                src_ref=send.at[order], dst_ref=recv.at[order], send_sem=send_sem,
                recv_sem=recv_sem.at[g], device_id=place_of(order, 1, here), device_id_type=MESH,
            ).start()
            return inner

        lax.fori_loop(jnp.maximum(first, 1), first + GROUP, start, 0)
        return carry

    lax.fori_loop(0, GROUPS, dispatch, 0)
    pltpu.make_async_copy(send.at[0], recv.at[0], recv_sem.at[0]).start()
    gate_copy.wait()
    up_copy.wait()

    def work(g, carry):
        at = pl.ds(g * GROUP, GROUP)
        first = g * GROUP
        whole = pl.ds(pl.multiple_of(g * PART, GROUP), PART)
        main = pl.ds(pl.multiple_of(g * PART, GROUP), ROWS)
        tail = pl.ds(pl.multiple_of(g * PART + ROWS, GROUP), GROUP)
        pltpu.make_async_copy(recv.at[at], recv.at[at], recv_sem.at[g]).wait()
        rows_in[main, :] = recv[at, :, 0:D].reshape(ROWS, D)
        x_last = dot(gather, recv[at, :, WIDE : WIDE + TAIL].reshape(ROWS, TAIL), NN).astype(bf16)
        for s in range(8):
            rows_in[tail, s * TAIL : (s + 1) * TAIL] = x_last[s * GROUP : (s + 1) * GROUP, :]
        h_last = dot(
            gather, recv[at, :, WIDE + TAIL : MESSAGE].reshape(ROWS, HEAD_SIZE), NN
        )
        h_last = jnp.concatenate([h_last[s * GROUP : (s + 1) * GROUP, :] for s in range(6)], axis=1)
        for n in range(3):
            tile = slice(n * 256, (n + 1) * 256)
            shifted = slice(FFE + n * 256, FFE + (n + 1) * 256)
            rows_grad = jnp.concatenate(
                [
                    recv[at, :, D + n * 256 : D + (n + 1) * 256].reshape(ROWS, 256).astype(f32),
                    h_last[:, tile],
                ],
                axis=0,
            )
            gate_pre = dot(rows_in[whole, :], weights[:, tile], NN)
            up_pre = dot(rows_in[whole, :], weights[:, shifted], NN)
            sig = jax.nn.sigmoid(gate_pre)
            gate_part = rows_grad * up_pre * sig * (1.0 + gate_pre * (1.0 - sig))
            parts[whole, tile] = gate_part.astype(bf16)
            parts[whole, shifted] = (rows_grad * gate_pre * sig).astype(bf16)

        def back_tile(n, inner):
            source = pl.ds(pl.multiple_of(n * 256, 256), 256)
            rows_back = dot(parts[whole, :], weights[source, :], NT).astype(bf16)
            back[at, :, source] = rows_back[:ROWS, :].reshape(GROUP, 8, 256)
            last_rows[pl.ds(pl.multiple_of(n * GROUP, GROUP), GROUP), :] = rows_back[ROWS:, :]
            return inner

        lax.fori_loop(0, 8, back_tile, 0)
        tails = dot(spread, last_rows[...], NN).astype(bf16)
        back[at, :, D : D + TAIL] = tails.reshape(GROUP, 8, TAIL)

        def start(order, inner):
            pltpu.make_async_remote_copy(
                src_ref=back.at[order], dst_ref=back_recv.at[order], send_sem=back_sem,
                recv_sem=back_recv_sem, device_id=place_of(order, -1, here), device_id_type=MESH,
            ).start()
            return inner

        lax.fori_loop(jnp.maximum(first, 1), first + GROUP, start, 0)
        return carry

    lax.fori_loop(0, GROUPS, work, 0)
    pltpu.make_async_copy(back.at[0], back_recv.at[0], back_recv_sem).start()

    def weight_grads(f, carry):
        tile = pl.ds(pl.multiple_of(f * 256, 256), 256)
        stage[tile, :] = dot(rows_in[:, tile], parts[...], TN).astype(bf16)
        pltpu.make_async_copy(
            stage.at[tile, pl.ds(0, FFE)], gate_out.at[tile, :], out_sem.at[0]
        ).start()
        pltpu.make_async_copy(
            stage.at[tile, pl.ds(FFE, FFE)], up_out.at[tile, :], out_sem.at[1]
        ).start()
        return carry

    lax.fori_loop(0, 8, weight_grads, 0)

    pltpu.make_async_copy(back_recv, back_recv, back_recv_sem).wait()
    slot_of = lax.rem(iota((tokens, 1024), 1), 8)
    state = state_ref[...].astype(f32)
    rstd = lax.rsqrt(jnp.mean(state * state, axis=-1, keepdims=True) + 1e-06)
    inner = jnp.zeros((tokens, 1), f32)
    weighted = []
    for n in range(8):
        tile = slice(n * 256, (n + 1) * 256)
        routed = dot(hot_t[:, 0:1024], back_recv[:, :, tile].reshape(1024, 256), NN)
        chosen = jnp.where(slot_of == n, hot_t[:, 1024:2048], jnp.zeros((), bf16))
        routed += dot(chosen, back_recv[:, :, D : D + TAIL].reshape(1024, TAIL), NN)
        weighted.append(gain[:, tile] * routed)
        inner += jnp.sum(weighted[n] * (state[:, tile] * rstd), axis=-1, keepdims=True)
    inner = inner * (1.0 / D)
    for n in range(8):
        tile = slice(n * 256, (n + 1) * 256)
        change = rstd * (weighted[n] - state[:, tile] * rstd * inner)
        residual_ref[:, tile] = (layer_ref[:, tile].astype(f32) + change).astype(bf16)

    pltpu.make_async_copy(stage.at[:, pl.ds(0, FFE)], gate_out, out_sem.at[0]).wait()
    pltpu.make_async_copy(stage.at[:, pl.ds(FFE, FFE)], up_out, out_sem.at[1]).wait()
    pltpu.make_async_copy(
        send.at[pl.ds(1, 127)], recv.at[pl.ds(1, 127)], send_sem
    ).wait()
    pltpu.make_async_copy(
        back.at[pl.ds(1, 127)], back_recv.at[pl.ds(1, 127)], back_sem
    ).wait()
    for copy in own:
        copy.wait()

    def finish_heads(step, carry):
        for copy in head_remote(step):
            copy.wait()
        return carry

    lax.fori_loop(1, 8, finish_heads, 0)


def expert_block(state, gain, layer_grad, grads, routes, w_gate, w_up, queries, keys, values):
    tokens = state.shape[0]
    bf16, f32 = jnp.bfloat16, jnp.float32
    vmem, hbm = pl.BlockSpec(memory_space=pltpu.VMEM), pl.BlockSpec(memory_space=pl.ANY)
    length = tokens * lax.axis_size("seq")
    dma = pltpu.SemaphoreType.DMA
    return pl.pallas_call(
        expert_kernel,
        out_shape=(
            jax.ShapeDtypeStruct((tokens, D), bf16),
            jax.ShapeDtypeStruct(w_gate.shape, bf16),
            jax.ShapeDtypeStruct(w_up.shape, bf16),
            jax.ShapeDtypeStruct((length, 512), bf16),
            jax.ShapeDtypeStruct((length, HEAD_SIZE), bf16),
            jax.ShapeDtypeStruct((length, HEAD_SIZE), bf16),
        ),
        in_specs=[vmem] * 5 + [hbm] * 5,
        out_specs=(vmem,) + (hbm,) * 5,
        scratch_shapes=[
            pltpu.VMEM((128, 8, MESSAGE), bf16),
            pltpu.VMEM((128, 8, MESSAGE), bf16),
            pltpu.VMEM((128, 8, D + TAIL), bf16),
            pltpu.VMEM((128, 8, D + TAIL), bf16),
            pltpu.VMEM((D, 2 * FFE), bf16),
            pltpu.VMEM((GROUPS * PART, D), bf16),
            pltpu.VMEM((GROUPS * PART, 2 * FFE), bf16),
            pltpu.VMEM((D, 2 * FFE), bf16),
            pltpu.VMEM((tokens, D), bf16),
            pltpu.VMEM((1024, tokens), bf16),
            pltpu.VMEM((tokens, 2048), bf16),
            pltpu.VMEM((128, tokens), bf16),
            pltpu.VMEM((1, tokens * TOP), f32),
            pltpu.VMEM((ROWS, TAIL), bf16),
            dma((2,)),
            dma,
            dma((GROUPS,)),
            dma,
            dma,
            dma((2,)),
            dma((3, 8)),
            dma((3, 8)),
        ],
        compiler_params=pltpu.CompilerParams(
            collective_id=1, has_side_effects=True, vmem_limit_bytes=60 << 20
        ),
        cost_estimate=pl.CostEstimate(
            flops=30_000_000_000, bytes_accessed=20_000_000, transcendentals=1_000_000
        ),
        name="expert_block",
    )(state, gain, layer_grad, grads, routes, w_gate, w_up, queries, keys, values)


def local(
    queries,
    keys,
    values,
    w_out,
    hidden_state,
    norm_gain,
    layer_grad,
    hidden_grad,
    routes,
    w_gate,
    w_up,
):
    residual_rows, gate_grad, up_grad, query_all, key_all, value_all = expert_block(
        hidden_state[0],
        norm_gain[None],
        layer_grad[0],
        hidden_grad[0].reshape(-1, FFE),
        routes[0],
        w_gate[0],
        w_up[0],
        queries[0],
        keys[0],
        values[0],
    )
    qkv = jnp.concatenate([query_all, key_all, value_all], axis=1)
    residual_all = lax.all_gather(residual_rows, "seq", axis=0, tiled=True)
    grads = attention_core(qkv, residual_all, w_out)
    query_out, key_out, value_out = return_heads(grads)
    return (query_out, key_out, value_out, residual_rows[None], gate_grad[None], up_grad[None])


def solution(mesh):
    return jax.shard_map(
        local,
        mesh=mesh,
        in_specs=(
            P("expert", "seq", None),
            P("expert", "seq", None),
            P("expert", "seq", None),
            P("seq", None),
            P("expert", "seq", None),
            P(),
            P("expert", "seq", None),
            P("expert", "seq", None, None),
            P("expert", "seq", None),
            P(("seq", "expert"), None, None),
            P(("seq", "expert"), None, None),
        ),
        out_specs=(
            P("expert", "seq", None),
            P("expert", "seq", None),
            P("expert", "seq", None),
            P("expert", "seq", None),
            P(("seq", "expert"), None, None),
            P(("seq", "expert"), None, None),
        ),
        check_vma=False,
    )
```

```python
import functools

import jax
import jax.numpy as jnp
from jax import lax
from jax.experimental import pallas as pl
from jax.experimental.pallas import tpu as pltpu
from jax.sharding import PartitionSpec as P

D = 2048
QUERY_HEADS = 32
KEY_VALUE_HEADS = 4
HEAD_SIZE = 128
FFE = 768
TOP = 8
LOG2E = 1.4426950408889634

NN = (((1,), (0,)), ((), ()))
NT = (((1,), (1,)), ((), ()))
TN = (((0,), (0,)), ((), ()))
MESH = pl.DeviceIdType.MESH


def dot(a, b, dims):
    return lax.dot_general(a, b, dims, preferred_element_type=jnp.float32)


def attention_kernel(
    residual_ref, w_hbm, query_hbm, key_hbm, value_hbm, query_out, key_out, value_out,
    gathered, w_out, queries, keys, values, grad, key_t, dk, dv, packed, returned,
    probs_0, probs_1, probs_2, probs_3, load_sem, gather_send, gather_recv,
    query_send, query_recv, pair_send, pair_recv,
):
    seq, expert = lax.axis_index("seq"), lax.axis_index("expert")
    x, c = seq // 2, lax.rem(seq, 2)
    tokens = residual_ref.shape[0]
    half = tokens // 2
    bf16, f32 = jnp.bfloat16, jnp.float32
    factor = HEAD_SIZE ** (-0.5)
    probs = (probs_0, probs_1, probs_2, probs_3)
    block = 2 * tokens

    def device(dx, dc):
        return lax.rem(x + dx, 4) * 2 + lax.rem(c + dc, 2)

    barrier = pltpu.get_barrier_semaphore()
    for step in range(1, 8):
        pl.semaphore_signal(
            barrier, inc=1, device_id=(device(step // 2, step % 2), expert), device_id_type=MESH
        )
    loads = [
        pltpu.make_async_copy(source, target, load_sem.at[n])
        for n, (source, target) in enumerate(
            ((query_hbm, queries), (key_hbm, keys), (value_hbm, values), (w_hbm, w_out))
        )
    ]
    for load in loads:
        load.start()

    def rows_of(owner, start, size):
        return pl.ds(pl.multiple_of(owner * tokens + start, size), size)

    def gather_copy(number, owner, start, size, to):
        rows = rows_of(owner, start, size)
        return pltpu.make_async_remote_copy(
            src_ref=gathered.at[rows, :], dst_ref=gathered.at[rows, :],
            send_sem=gather_send.at[number], recv_sem=gather_recv.at[number],
            device_id=(to, expert), device_id_type=MESH,
        )

    own, left, right, far = device(0, 0), device(3, 0), device(1, 0), device(2, 0)
    mate = device(0, 1)
    gathered[rows_of(own, 0, tokens), :] = residual_ref[...]
    pl.semaphore_wait(barrier, 7)
    copies = [
        gather_copy(0, own, 0, half, right),
        gather_copy(1, own, half, half, left),
        gather_copy(2, own, half, half, right),
        gather_copy(3, own, 0, half, left),
        gather_copy(4, own, 0, tokens, mate),
        gather_copy(5, left, 0, half, right),
        gather_copy(6, right, half, half, left),
        gather_copy(7, left, 0, half, mate),
        gather_copy(8, right, half, half, mate),
        gather_copy(9, left, half, half, mate),
        gather_copy(10, right, 0, half, mate),
        gather_copy(11, far, 0, half, mate),
        gather_copy(12, far, half, half, mate),
    ]
    for copy in copies[:5]:
        copy.start()
    for load in loads:
        load.wait()

    key_t[...] = keys[...].astype(f32).T.astype(bf16)
    dk[...] = jnp.zeros_like(dk)
    dv[...] = jnp.zeros_like(dv)

    def softmax_block(i):
        lower, upper = i * block, (i + 1) * block
        key_pos = lax.broadcasted_iota(jnp.int32, (block, block), 0)
        query_pos = lax.broadcasted_iota(jnp.int32, (block, block), 1)
        for head in range(4):
            columns = slice(head * HEAD_SIZE, (head + 1) * HEAD_SIZE)
            scores = dot(keys[0:upper, :], queries[lower:upper, columns], NT) * (factor * LOG2E)
            diagonal = jnp.where(key_pos <= query_pos, scores[lower:upper], -1e30)
            scores = diagonal if i == 0 else jnp.concatenate([scores[:lower], diagonal], axis=0)
            exps = jnp.exp2(scores - jnp.max(scores, axis=0, keepdims=True))
            probs[i][head, :, :] = exps * (1.0 / jnp.sum(exps, axis=0, keepdims=True))

    def project(owner):
        rows = rows_of(owner, 0, tokens)
        grad[rows, :] = dot(gathered[rows, :], w_out[...], NT).astype(bf16)

    softmax_block(0)
    softmax_block(1)
    copies[0].wait_recv()
    copies[5].start()
    copies[7].start()
    copies[1].wait_recv()
    copies[6].start()
    copies[8].start()
    softmax_block(2)
    copies[2].wait_recv()
    copies[9].start()
    copies[3].wait_recv()
    copies[10].start()
    softmax_block(3)
    project(own)
    copies[4].wait_recv()
    project(mate)
    project(left)
    project(right)
    copies[5].wait_recv()
    copies[11].start()
    copies[6].wait_recv()
    copies[12].start()
    project(far)
    for copy in copies[7:11]:
        copy.wait_recv()
    project(device(3, 1))
    project(device(1, 1))
    for copy in copies[11:]:
        copy.wait_recv()
    project(device(2, 1))

    def backward_block(i):
        lower, upper = i * block, (i + 1) * block
        for head in range(4):
            columns = slice(head * HEAD_SIZE, (head + 1) * HEAD_SIZE)
            out_grad = grad[lower:upper, columns]
            prob = probs[i][head]
            dv[0:upper, :] += dot(prob.astype(bf16), out_grad, NN)
            prob_grad = dot(values[0:upper, :], out_grad, NT)
            delta = jnp.sum(prob * prob_grad, axis=0, keepdims=True)
            score_grad = (prob * (prob_grad - delta)).astype(bf16)
            dk[0:upper, :] += dot(score_grad, queries[lower:upper, columns], NN)
            query_grad = dot(key_t[:, 0:upper], score_grad, NN) * factor
            packed[lower:upper, columns] = query_grad.T.astype(bf16)

    pair = slice(4 * HEAD_SIZE, 6 * HEAD_SIZE)

    def query_copy(dx, dc):
        to, number = device(dx, dc), dx * 2 + dc
        return pltpu.make_async_remote_copy(
            src_ref=packed.at[rows_of(to, 0, tokens), pl.ds(0, 512)],
            dst_ref=query_out.at[:, pl.ds(pl.multiple_of(seq * 512, 512), 512)],
            send_sem=query_send.at[number], recv_sem=query_recv.at[number],
            device_id=(to, expert), device_id_type=MESH,
        )

    def pair_copy(dx, dc):
        to, number = device(dx, dc), dx * 2 + dc
        return pltpu.make_async_remote_copy(
            src_ref=packed.at[rows_of(to, 0, tokens), pl.ds(512, 256)],
            dst_ref=returned.at[seq],
            send_sem=pair_send.at[number], recv_sem=pair_recv.at[number],
            device_id=(to, expert), device_id_type=MESH,
        )

    own_query = pltpu.make_async_copy(
        packed.at[rows_of(seq, 0, tokens), pl.ds(0, 512)],
        query_out.at[:, pl.ds(pl.multiple_of(seq * 512, 512), 512)],
        query_send.at[0],
    )

    def backward_step(step, carry):
        dx = lax.rem(step + 1, 4)
        chip = lax.rem(x + dx, 4)
        for i in range(4):
            pl.when(chip == i)(functools.partial(backward_block, i))

        @pl.when(step < 3)
        def _():
            query_copy(dx, 0).start()

        @pl.when(step == 3)
        def _():
            own_query.start()

        query_copy(dx, 1).start()
        return carry

    lax.fori_loop(0, 4, backward_step, 0)
    packed[:, 512:640] = (dk[...] * factor).astype(bf16)
    packed[:, 640:768] = dv[...].astype(bf16)
    for step in (2, 3, 4, 5, 6, 7, 1):
        pair_copy(step // 2, step % 2).start()
    returned[seq, :, :] = packed[rows_of(seq, 0, tokens), pair]
    for step in range(1, 8):
        pair_copy(step // 2, step % 2).wait_recv()
    for head in range(KEY_VALUE_HEADS):
        total = returned[2 * head].astype(f32) + returned[2 * head + 1].astype(f32)
        columns = slice(head * HEAD_SIZE, (head + 1) * HEAD_SIZE)
        key_out[:, columns] = total[:, 0:HEAD_SIZE].astype(bf16)
        value_out[:, columns] = total[:, HEAD_SIZE:].astype(bf16)
    for copy in copies:
        copy.wait_send()
    for step in range(1, 8):
        query_copy(step // 2, step % 2).wait()
        pair_copy(step // 2, step % 2).wait_send()
    own_query.wait()


def attention_core(residual, w_out, queries, keys, values):
    tokens, length = residual.shape[0], queries.shape[0]
    bf16, f32 = jnp.bfloat16, jnp.float32
    vmem, hbm = pl.BlockSpec(memory_space=pltpu.VMEM), pl.BlockSpec(memory_space=pl.ANY)
    dma = pltpu.SemaphoreType.DMA
    return pl.pallas_call(
        attention_kernel,
        out_shape=(
            jax.ShapeDtypeStruct((tokens, QUERY_HEADS * HEAD_SIZE), bf16),
            jax.ShapeDtypeStruct((tokens, KEY_VALUE_HEADS * HEAD_SIZE), bf16),
            jax.ShapeDtypeStruct((tokens, KEY_VALUE_HEADS * HEAD_SIZE), bf16),
        ),
        in_specs=[vmem] + [hbm] * 4,
        out_specs=(hbm, vmem, vmem),
        scratch_shapes=[
            pltpu.VMEM((length, D), bf16),
            pltpu.VMEM(w_out.shape, bf16),
            pltpu.VMEM(queries.shape, bf16),
            pltpu.VMEM(keys.shape, bf16),
            pltpu.VMEM(values.shape, bf16),
            pltpu.VMEM((length, 512), bf16),
            pltpu.VMEM((HEAD_SIZE, length), bf16),
            pltpu.VMEM((length, HEAD_SIZE), f32),
            pltpu.VMEM((length, HEAD_SIZE), f32),
            pltpu.VMEM((length, 768), bf16),
            pltpu.VMEM((8, tokens, 256), bf16),
            pltpu.VMEM((4, 256, 256), f32),
            pltpu.VMEM((4, 512, 256), f32),
            pltpu.VMEM((4, 768, 256), f32),
            pltpu.VMEM((4, 1024, 256), f32),
            dma((4,)),
            dma((13,)),
            dma((13,)),
            dma((8,)),
            dma((8,)),
            dma((8,)),
            dma((8,)),
        ],
        compiler_params=pltpu.CompilerParams(
            collective_id=2, has_side_effects=True, vmem_limit_bytes=56 << 20
        ),
        cost_estimate=pl.CostEstimate(
            flops=9_000_000_000, bytes_accessed=10_000_000, transcendentals=3_000_000
        ),
        name="attention_core",
    )(residual, w_out, queries, keys, values)


ORDER = 37
GROUP = 32
GROUPS = 4
ROWS = GROUP * 8
PART = ROWS + GROUP
TAIL = D // 8
WIDE = D + FFE
MESSAGE = WIDE + TAIL + HEAD_SIZE


def place_of(order, sign, here):
    x, c, y, z = here
    code = lax.rem(order * ORDER, 128)
    dc, dx, dy, dz = lax.rem(code, 2), lax.rem(code // 2, 4), lax.rem(code // 8, 4), code // 32
    if sign < 0:
        dx, dy, dz = 4 - dx, 4 - dy, 4 - dz
    return (
        lax.rem(x + dx, 4) * 2 + lax.rem(c + dc, 2),
        lax.rem(y + dy, 4) * 4 + lax.rem(z + dz, 4),
    )


def expert_of(order, here):
    seq, expert = place_of(order, 1, here)
    return seq * 16 + expert


def expert_kernel(
    state_ref, gain_ref, layer_ref, grads_ref, routes_ref, gate_hbm, up_hbm, query_hbm, key_hbm,
    value_hbm, residual_ref, gate_out, up_out, query_all, key_all, value_all,
    send, recv, back, back_recv, weights, rows_in, parts, stage, expert_in, hot, hot_t, last,
    codes, last_rows, weight_sem, send_sem, recv_sem, back_sem, back_recv_sem, out_sem,
    head_send, head_recv,
):
    seq, expert = lax.axis_index("seq"), lax.axis_index("expert")
    here = (seq // 2, lax.rem(seq, 2), expert // 4, lax.rem(expert, 4))
    tokens = state_ref.shape[0]
    bf16, f32 = jnp.bfloat16, jnp.float32

    def iota(shape, axis):
        return lax.broadcasted_iota(jnp.int32, shape, axis)

    barrier = pltpu.get_barrier_semaphore()

    def greet(order, carry):
        pl.semaphore_signal(barrier, inc=1, device_id=place_of(order, 1, here), device_id_type=MESH)
        return carry

    lax.fori_loop(1, 128, greet, 0)
    gate_copy = pltpu.make_async_copy(gate_hbm, weights.at[:, pl.ds(0, FFE)], weight_sem.at[0])
    up_copy = pltpu.make_async_copy(up_hbm, weights.at[:, pl.ds(FFE, FFE)], weight_sem.at[1])
    gate_copy.start()
    up_copy.start()

    gain = gain_ref[...].astype(f32)
    gain = jnp.concatenate([gain[j : j + 1, :] for j in range(D // 128)], axis=1)
    state = state_ref[...].astype(f32)
    rstd = lax.rsqrt(jnp.mean(state * state, axis=-1, keepdims=True) + 1e-06)
    expert_in[...] = (state * rstd * gain).astype(bf16)

    lanes = iota((tokens, 128), 1)
    route = routes_ref[...].astype(f32).T
    named = [route[:, k : k + 1] == lanes.astype(f32) for k in range(TOP)]
    count = sum(jnp.where(n, 1.0, 0.0) for n in named)
    earlier = jnp.where(iota((tokens, tokens), 0) > iota((tokens, tokens), 1), 1.0, 0.0)
    rank = dot(earlier.astype(bf16), count.astype(bf16), NN)
    columns = iota((tokens, tokens * TOP), 1) - iota((tokens, tokens * TOP), 0) * TOP
    spread_codes = jnp.zeros((tokens, tokens * TOP), f32)
    for k in range(TOP):
        route_rank = jnp.sum(jnp.where(named[k], rank, 0.0), axis=1, keepdims=True)
        code = route[:, k : k + 1] * 16.0 + route_rank
        spread_codes = jnp.where(columns == k, code, spread_codes)
    codes[...] = jnp.sum(spread_codes, axis=0, keepdims=True)
    target = expert_of(iota((128, 128), 0), here)
    ordered = jnp.where(target == iota((128, 128), 1), 1.0, 0.0).astype(bf16)
    rank_t = dot(ordered, jnp.where(count > 0.0, rank, -1.0).astype(bf16), NT)
    slot = iota((128, 8, tokens), 1).astype(f32)
    rank_wide = jnp.broadcast_to(rank_t[:, None, :], (128, 8, tokens))
    hot_full = jnp.where(rank_wide == slot, 1.0, 0.0).reshape(1024, tokens)
    hot[...] = hot_full.astype(bf16)
    hot_t[:, 0:1024] = hot_full.T.astype(bf16)
    last_full = jnp.where(rank_wide == 8.0, 1.0, 0.0).reshape(1024, tokens)
    hot_t[:, 1024:2048] = last_full.T.astype(bf16)
    last[...] = jnp.where(rank_t == 8.0, 1.0, 0.0).astype(bf16)

    row, col = iota((ROWS, ROWS), 0), iota((ROWS, ROWS), 1)
    spread = jnp.where(col == lax.rem(row, 8) * GROUP + row // 8, 1.0, 0.0).astype(bf16)
    gather = jnp.where(row == lax.rem(col, 8) * GROUP + col // 8, 1.0, 0.0).astype(bf16)

    pl.semaphore_wait(barrier, 127)

    def head_copies(step):
        dx, dc = step // 2, lax.rem(step, 2)
        to = lax.rem(here[0] + dx, 4) * 2 + lax.rem(here[1] + dc, 2)
        rows = pl.ds(pl.multiple_of(seq * tokens, tokens), tokens)
        wide = pl.ds(pl.multiple_of(to * 512, 512), 512)
        narrow = pl.ds(pl.multiple_of(to // 2 * HEAD_SIZE, HEAD_SIZE), HEAD_SIZE)
        return to, (
            (query_hbm.at[:, wide], query_all.at[rows, :]),
            (key_hbm.at[:, narrow], key_all.at[rows, :]),
            (value_hbm.at[:, narrow], value_all.at[rows, :]),
        )

    def head_remote(step):
        to, pairs = head_copies(step)
        return [
            pltpu.make_async_remote_copy(
                src_ref=source, dst_ref=target_ref, send_sem=head_send.at[n, step],
                recv_sem=head_recv.at[n, step], device_id=(to, expert), device_id_type=MESH,
            )
            for n, (source, target_ref) in enumerate(pairs)
        ]

    own = [
        pltpu.make_async_copy(source, target_ref, head_send.at[n, 0])
        for n, (source, target_ref) in enumerate(head_copies(0)[1])
    ]
    for copy in own:
        copy.start()

    def send_heads(step, carry):
        for copy in head_remote(step):
            copy.start()
        return carry

    lax.fori_loop(1, 8, send_heads, 0)

    def dispatch(g, carry):
        at = pl.ds(g * GROUP, GROUP)
        rows = pl.ds(pl.multiple_of(g * ROWS, ROWS), ROWS)
        first = g * GROUP
        x_rows = dot(hot[rows, :], expert_in[...], NN).astype(bf16)
        send[at, :, 0:D] = x_rows.reshape(GROUP, 8, D)
        number = iota((ROWS, 128), 0)
        row_code = (expert_of(first + number // 8, here) * 16 + lax.rem(number, 8)).astype(f32)
        last_code = (expert_of(first + iota((GROUP, 128), 0), here) * 16 + 8).astype(f32)

        def one_hot(code):
            pieces = [
                jnp.where(codes[:, j * 128 : (j + 1) * 128] == code, 1.0, 0.0).astype(bf16)
                for j in range(TOP)
            ]
            return jnp.concatenate(pieces, axis=1)

        h_rows = dot(one_hot(row_code), grads_ref[...], NN).astype(bf16)
        send[at, :, D:WIDE] = h_rows.reshape(GROUP, 8, FFE)
        x_last = dot(last[pl.ds(pl.multiple_of(first, GROUP), GROUP), :], expert_in[...], NN)
        x_last = x_last.astype(bf16)
        h_last = dot(one_hot(last_code), grads_ref[...], NN).astype(bf16)
        x_stack = jnp.concatenate([x_last[:, s * TAIL : (s + 1) * TAIL] for s in range(8)], axis=0)
        h_stack = jnp.concatenate([h_last[:, s * 128 : (s + 1) * 128] for s in range(6)], axis=0)
        x_tail = dot(spread, x_stack, NN).astype(bf16)
        h_tail = dot(spread[:, 0 : 6 * GROUP], h_stack, NN).astype(bf16)
        send[at, :, WIDE : WIDE + TAIL] = x_tail.reshape(GROUP, 8, TAIL)
        send[at, :, WIDE + TAIL : MESSAGE] = h_tail.reshape(GROUP, 8, HEAD_SIZE)

        def start(order, inner):
            pltpu.make_async_remote_copy(
                src_ref=send.at[order], dst_ref=recv.at[order], send_sem=send_sem,
                recv_sem=recv_sem.at[g], device_id=place_of(order, 1, here), device_id_type=MESH,
            ).start()
            return inner

        lax.fori_loop(jnp.maximum(first, 1), first + GROUP, start, 0)
        return carry

    lax.fori_loop(0, GROUPS, dispatch, 0)
    pltpu.make_async_copy(send.at[0], recv.at[0], recv_sem.at[0]).start()
    gate_copy.wait()
    up_copy.wait()

    def work(g, carry):
        at = pl.ds(g * GROUP, GROUP)
        first = g * GROUP
        whole = pl.ds(pl.multiple_of(g * PART, GROUP), PART)
        main = pl.ds(pl.multiple_of(g * PART, GROUP), ROWS)
        tail = pl.ds(pl.multiple_of(g * PART + ROWS, GROUP), GROUP)
        pltpu.make_async_copy(recv.at[at], recv.at[at], recv_sem.at[g]).wait()
        rows_in[main, :] = recv[at, :, 0:D].reshape(ROWS, D)
        x_last = dot(gather, recv[at, :, WIDE : WIDE + TAIL].reshape(ROWS, TAIL), NN).astype(bf16)
        for s in range(8):
            rows_in[tail, s * TAIL : (s + 1) * TAIL] = x_last[s * GROUP : (s + 1) * GROUP, :]
        h_last = dot(
            gather, recv[at, :, WIDE + TAIL : MESSAGE].reshape(ROWS, HEAD_SIZE), NN
        )
        h_last = jnp.concatenate([h_last[s * GROUP : (s + 1) * GROUP, :] for s in range(6)], axis=1)
        for n in range(3):
            tile = slice(n * 256, (n + 1) * 256)
            shifted = slice(FFE + n * 256, FFE + (n + 1) * 256)
            rows_grad = jnp.concatenate(
                [
                    recv[at, :, D + n * 256 : D + (n + 1) * 256].reshape(ROWS, 256).astype(f32),
                    h_last[:, tile],
                ],
                axis=0,
            )
            gate_pre = dot(rows_in[whole, :], weights[:, tile], NN)
            up_pre = dot(rows_in[whole, :], weights[:, shifted], NN)
            sig = jax.nn.sigmoid(gate_pre)
            gate_part = rows_grad * up_pre * sig * (1.0 + gate_pre * (1.0 - sig))
            parts[whole, tile] = gate_part.astype(bf16)
            parts[whole, shifted] = (rows_grad * gate_pre * sig).astype(bf16)

        def back_tile(n, inner):
            source = pl.ds(pl.multiple_of(n * 256, 256), 256)
            rows_back = dot(parts[whole, :], weights[source, :], NT).astype(bf16)
            back[at, :, source] = rows_back[:ROWS, :].reshape(GROUP, 8, 256)
            last_rows[pl.ds(pl.multiple_of(n * GROUP, GROUP), GROUP), :] = rows_back[ROWS:, :]
            return inner

        lax.fori_loop(0, 8, back_tile, 0)
        tails = dot(spread, last_rows[...], NN).astype(bf16)
        back[at, :, D : D + TAIL] = tails.reshape(GROUP, 8, TAIL)

        def start(order, inner):
            pltpu.make_async_remote_copy(
                src_ref=back.at[order], dst_ref=back_recv.at[order], send_sem=back_sem,
                recv_sem=back_recv_sem, device_id=place_of(order, -1, here), device_id_type=MESH,
            ).start()
            return inner

        lax.fori_loop(jnp.maximum(first, 1), first + GROUP, start, 0)
        return carry

    lax.fori_loop(0, GROUPS, work, 0)
    pltpu.make_async_copy(back.at[0], back_recv.at[0], back_recv_sem).start()

    def weight_grads(f, carry):
        tile = pl.ds(pl.multiple_of(f * 256, 256), 256)
        stage[tile, :] = dot(rows_in[:, tile], parts[...], TN).astype(bf16)
        pltpu.make_async_copy(
            stage.at[tile, pl.ds(0, FFE)], gate_out.at[tile, :], out_sem.at[0]
        ).start()
        pltpu.make_async_copy(
            stage.at[tile, pl.ds(FFE, FFE)], up_out.at[tile, :], out_sem.at[1]
        ).start()
        return carry

    lax.fori_loop(0, 8, weight_grads, 0)

    pltpu.make_async_copy(back_recv, back_recv, back_recv_sem).wait()
    slot_of = lax.rem(iota((tokens, 1024), 1), 8)
    state = state_ref[...].astype(f32)
    rstd = lax.rsqrt(jnp.mean(state * state, axis=-1, keepdims=True) + 1e-06)
    inner = jnp.zeros((tokens, 1), f32)
    weighted = []
    for n in range(8):
        tile = slice(n * 256, (n + 1) * 256)
        routed = dot(hot_t[:, 0:1024], back_recv[:, :, tile].reshape(1024, 256), NN)
        chosen = jnp.where(slot_of == n, hot_t[:, 1024:2048], jnp.zeros((), bf16))
        routed += dot(chosen, back_recv[:, :, D : D + TAIL].reshape(1024, TAIL), NN)
        weighted.append(gain[:, tile] * routed)
        inner += jnp.sum(weighted[n] * (state[:, tile] * rstd), axis=-1, keepdims=True)
    inner = inner * (1.0 / D)
    for n in range(8):
        tile = slice(n * 256, (n + 1) * 256)
        change = rstd * (weighted[n] - state[:, tile] * rstd * inner)
        residual_ref[:, tile] = (layer_ref[:, tile].astype(f32) + change).astype(bf16)

    pltpu.make_async_copy(stage.at[:, pl.ds(0, FFE)], gate_out, out_sem.at[0]).wait()
    pltpu.make_async_copy(stage.at[:, pl.ds(FFE, FFE)], up_out, out_sem.at[1]).wait()
    pltpu.make_async_copy(
        send.at[pl.ds(1, 127)], recv.at[pl.ds(1, 127)], send_sem
    ).wait()
    pltpu.make_async_copy(
        back.at[pl.ds(1, 127)], back_recv.at[pl.ds(1, 127)], back_sem
    ).wait()
    for copy in own:
        copy.wait()

    def finish_heads(step, carry):
        for copy in head_remote(step):
            copy.wait()
        return carry

    lax.fori_loop(1, 8, finish_heads, 0)


def expert_block(state, gain, layer_grad, grads, routes, w_gate, w_up, queries, keys, values):
    tokens = state.shape[0]
    bf16, f32 = jnp.bfloat16, jnp.float32
    vmem, hbm = pl.BlockSpec(memory_space=pltpu.VMEM), pl.BlockSpec(memory_space=pl.ANY)
    length = tokens * lax.axis_size("seq")
    dma = pltpu.SemaphoreType.DMA
    return pl.pallas_call(
        expert_kernel,
        out_shape=(
            jax.ShapeDtypeStruct((tokens, D), bf16),
            jax.ShapeDtypeStruct(w_gate.shape, bf16),
            jax.ShapeDtypeStruct(w_up.shape, bf16),
            jax.ShapeDtypeStruct((length, 512), bf16),
            jax.ShapeDtypeStruct((length, HEAD_SIZE), bf16),
            jax.ShapeDtypeStruct((length, HEAD_SIZE), bf16),
        ),
        in_specs=[vmem] * 5 + [hbm] * 5,
        out_specs=(vmem,) + (hbm,) * 5,
        scratch_shapes=[
            pltpu.VMEM((128, 8, MESSAGE), bf16),
            pltpu.VMEM((128, 8, MESSAGE), bf16),
            pltpu.VMEM((128, 8, D + TAIL), bf16),
            pltpu.VMEM((128, 8, D + TAIL), bf16),
            pltpu.VMEM((D, 2 * FFE), bf16),
            pltpu.VMEM((GROUPS * PART, D), bf16),
            pltpu.VMEM((GROUPS * PART, 2 * FFE), bf16),
            pltpu.VMEM((D, 2 * FFE), bf16),
            pltpu.VMEM((tokens, D), bf16),
            pltpu.VMEM((1024, tokens), bf16),
            pltpu.VMEM((tokens, 2048), bf16),
            pltpu.VMEM((128, tokens), bf16),
            pltpu.VMEM((1, tokens * TOP), f32),
            pltpu.VMEM((ROWS, TAIL), bf16),
            dma((2,)),
            dma,
            dma((GROUPS,)),
            dma,
            dma,
            dma((2,)),
            dma((3, 8)),
            dma((3, 8)),
        ],
        compiler_params=pltpu.CompilerParams(
            collective_id=1, has_side_effects=True, vmem_limit_bytes=60 << 20
        ),
        cost_estimate=pl.CostEstimate(
            flops=30_000_000_000, bytes_accessed=20_000_000, transcendentals=1_000_000
        ),
        name="expert_block",
    )(state, gain, layer_grad, grads, routes, w_gate, w_up, queries, keys, values)


def local(
    queries,
    keys,
    values,
    w_out,
    hidden_state,
    norm_gain,
    layer_grad,
    hidden_grad,
    routes,
    w_gate,
    w_up,
):
    residual_rows, gate_grad, up_grad, query_all, key_all, value_all = expert_block(
        hidden_state[0],
        norm_gain.reshape(D // 128, 128),
        layer_grad[0],
        hidden_grad[0].reshape(-1, FFE),
        routes[0].T,
        w_gate[0],
        w_up[0],
        queries[0],
        keys[0],
        values[0],
    )
    query_out, key_out, value_out = attention_core(
        residual_rows, w_out, query_all, key_all, value_all
    )
    return (query_out[None], key_out[None], value_out[None], residual_rows[None], gate_grad[None], up_grad[None])


def solution(mesh):
    return jax.shard_map(
        local,
        mesh=mesh,
        in_specs=(
            P("expert", "seq", None),
            P("expert", "seq", None),
            P("expert", "seq", None),
            P("seq", None),
            P("expert", "seq", None),
            P(),
            P("expert", "seq", None),
            P("expert", "seq", None, None),
            P("expert", "seq", None),
            P(("seq", "expert"), None, None),
            P(("seq", "expert"), None, None),
        ),
        out_specs=(
            P("expert", "seq", None),
            P("expert", "seq", None),
            P("expert", "seq", None),
            P("expert", "seq", None),
            P(("seq", "expert"), None, None),
            P(("seq", "expert"), None, None),
        ),
        check_vma=False,
    )
```

```python
import functools

import jax
import jax.numpy as jnp
from jax import lax
from jax.experimental import pallas as pl
from jax.experimental.pallas import tpu as pltpu
from jax.sharding import PartitionSpec as P

D = 2048
QUERY_HEADS = 32
KEY_VALUE_HEADS = 4
HEAD_SIZE = 128
FFE = 768
TOP = 8
LOG2E = 1.4426950408889634

NN = (((1,), (0,)), ((), ()))
NT = (((1,), (1,)), ((), ()))
TN = (((0,), (0,)), ((), ()))
MESH = pl.DeviceIdType.MESH


def dot(a, b, dims):
    return lax.dot_general(a, b, dims, preferred_element_type=jnp.float32)


def attention_kernel(
    residual_ref, w_hbm, query_hbm, key_hbm, value_hbm, query_out, key_out, value_out,
    gathered, w_out, queries, keys, values, grad, key_t, dk, dv, packed, returned,
    probs_0, probs_1, probs_2, probs_3, load_sem, gather_send, gather_recv,
    query_send, query_recv, pair_send, pair_recv,
):
    seq, expert = lax.axis_index("seq"), lax.axis_index("expert")
    x, c = seq // 2, lax.rem(seq, 2)
    tokens = residual_ref.shape[0]
    half = tokens // 2
    bf16, f32 = jnp.bfloat16, jnp.float32
    factor = HEAD_SIZE ** (-0.5)
    probs = (probs_0, probs_1, probs_2, probs_3)
    block = 2 * tokens

    def device(dx, dc):
        return lax.rem(x + dx, 4) * 2 + lax.rem(c + dc, 2)

    barrier = pltpu.get_barrier_semaphore()
    for step in range(1, 8):
        pl.semaphore_signal(
            barrier, inc=1, device_id=(device(step // 2, step % 2), expert), device_id_type=MESH
        )
    loads = [
        pltpu.make_async_copy(source, target, load_sem.at[n])
        for n, (source, target) in enumerate(
            ((query_hbm, queries), (key_hbm, keys), (value_hbm, values), (w_hbm, w_out))
        )
    ]
    for load in loads:
        load.start()

    def rows_of(owner, start, size):
        return pl.ds(pl.multiple_of(owner * tokens + start, size), size)

    def gather_copy(number, owner, start, size, to):
        rows = rows_of(owner, start, size)
        return pltpu.make_async_remote_copy(
            src_ref=gathered.at[rows, :], dst_ref=gathered.at[rows, :],
            send_sem=gather_send.at[number], recv_sem=gather_recv.at[number],
            device_id=(to, expert), device_id_type=MESH,
        )

    own, left, right, far = device(0, 0), device(3, 0), device(1, 0), device(2, 0)
    mate = device(0, 1)
    gathered[rows_of(own, 0, tokens), :] = residual_ref[...]
    pl.semaphore_wait(barrier, 7)
    copies = [
        gather_copy(0, own, 0, half, right),
        gather_copy(1, own, half, half, left),
        gather_copy(2, own, half, half, right),
        gather_copy(3, own, 0, half, left),
        gather_copy(4, own, 0, tokens, mate),
        gather_copy(5, left, 0, half, right),
        gather_copy(6, right, half, half, left),
        gather_copy(7, left, 0, half, mate),
        gather_copy(8, right, half, half, mate),
        gather_copy(9, left, half, half, mate),
        gather_copy(10, right, 0, half, mate),
        gather_copy(11, far, 0, half, mate),
        gather_copy(12, far, half, half, mate),
    ]
    for copy in copies[:5]:
        copy.start()
    for load in loads:
        load.wait()

    key_t[...] = keys[...].astype(f32).T.astype(bf16)
    dk[...] = jnp.zeros_like(dk)
    dv[...] = jnp.zeros_like(dv)

    def softmax_block(i):
        lower, upper = i * block, (i + 1) * block
        key_pos = lax.broadcasted_iota(jnp.int32, (block, block), 0)
        query_pos = lax.broadcasted_iota(jnp.int32, (block, block), 1)
        for head in range(4):
            columns = slice(head * HEAD_SIZE, (head + 1) * HEAD_SIZE)
            scores = dot(keys[0:upper, :], queries[lower:upper, columns], NT) * (factor * LOG2E)
            diagonal = jnp.where(key_pos <= query_pos, scores[lower:upper], -1e30)
            scores = diagonal if i == 0 else jnp.concatenate([scores[:lower], diagonal], axis=0)
            exps = jnp.exp2(scores - jnp.max(scores, axis=0, keepdims=True))
            probs[i][head, :, :] = exps * (1.0 / jnp.sum(exps, axis=0, keepdims=True))

    def project(owner):
        rows = rows_of(owner, 0, tokens)
        grad[rows, :] = dot(gathered[rows, :], w_out[...], NT).astype(bf16)

    softmax_block(0)
    softmax_block(1)
    copies[0].wait_recv()
    copies[5].start()
    copies[7].start()
    copies[1].wait_recv()
    copies[6].start()
    copies[8].start()
    softmax_block(2)
    copies[2].wait_recv()
    copies[9].start()
    copies[3].wait_recv()
    copies[10].start()
    softmax_block(3)
    project(own)
    copies[4].wait_recv()
    project(mate)
    project(left)
    project(right)
    copies[5].wait_recv()
    copies[11].start()
    copies[6].wait_recv()
    copies[12].start()
    project(far)
    for copy in copies[7:11]:
        copy.wait_recv()
    project(device(3, 1))
    project(device(1, 1))
    for copy in copies[11:]:
        copy.wait_recv()
    project(device(2, 1))

    def backward_block(i):
        lower, upper = i * block, (i + 1) * block
        for head in range(4):
            columns = slice(head * HEAD_SIZE, (head + 1) * HEAD_SIZE)
            out_grad = grad[lower:upper, columns]
            prob = probs[i][head]
            dv[0:upper, :] += dot(prob.astype(bf16), out_grad, NN)
            prob_grad = dot(values[0:upper, :], out_grad, NT)
            delta = jnp.sum(prob * prob_grad, axis=0, keepdims=True)
            score_grad = (prob * (prob_grad - delta)).astype(bf16)
            dk[0:upper, :] += dot(score_grad, queries[lower:upper, columns], NN)
            query_grad = dot(key_t[:, 0:upper], score_grad, NN) * factor
            packed[lower:upper, columns] = query_grad.T.astype(bf16)

    pair = slice(4 * HEAD_SIZE, 6 * HEAD_SIZE)

    def query_copy(dx, dc):
        to, number = device(dx, dc), dx * 2 + dc
        return pltpu.make_async_remote_copy(
            src_ref=packed.at[rows_of(to, 0, tokens), pl.ds(0, 512)],
            dst_ref=query_out.at[:, pl.ds(pl.multiple_of(seq * 512, 512), 512)],
            send_sem=query_send.at[number], recv_sem=query_recv.at[number],
            device_id=(to, expert), device_id_type=MESH,
        )

    def pair_copy(dx, dc):
        to, number = device(dx, dc), dx * 2 + dc
        return pltpu.make_async_remote_copy(
            src_ref=packed.at[rows_of(to, 0, tokens), pl.ds(512, 256)],
            dst_ref=returned.at[seq],
            send_sem=pair_send.at[number], recv_sem=pair_recv.at[number],
            device_id=(to, expert), device_id_type=MESH,
        )

    own_query = pltpu.make_async_copy(
        packed.at[rows_of(seq, 0, tokens), pl.ds(0, 512)],
        query_out.at[:, pl.ds(pl.multiple_of(seq * 512, 512), 512)],
        query_send.at[0],
    )

    def backward_step(step, carry):
        dx = lax.rem(step + 1, 4)
        chip = lax.rem(x + dx, 4)
        for i in range(4):
            pl.when(chip == i)(functools.partial(backward_block, i))

        @pl.when(step < 3)
        def _():
            query_copy(dx, 0).start()

        @pl.when(step == 3)
        def _():
            own_query.start()

        query_copy(dx, 1).start()
        return carry

    lax.fori_loop(0, 4, backward_step, 0)
    packed[:, 512:640] = (dk[...] * factor).astype(bf16)
    packed[:, 640:768] = dv[...].astype(bf16)
    for step in (2, 3, 4, 5, 6, 7, 1):
        pair_copy(step // 2, step % 2).start()
    returned[seq, :, :] = packed[rows_of(seq, 0, tokens), pair]
    for step in range(1, 8):
        pair_copy(step // 2, step % 2).wait_recv()
    for head in range(KEY_VALUE_HEADS):
        total = returned[2 * head].astype(f32) + returned[2 * head + 1].astype(f32)
        columns = slice(head * HEAD_SIZE, (head + 1) * HEAD_SIZE)
        key_out[:, columns] = total[:, 0:HEAD_SIZE].astype(bf16)
        value_out[:, columns] = total[:, HEAD_SIZE:].astype(bf16)
    for copy in copies:
        copy.wait_send()
    for step in range(1, 8):
        query_copy(step // 2, step % 2).wait()
        pair_copy(step // 2, step % 2).wait_send()
    own_query.wait()


def attention_core(residual, w_out, queries, keys, values):
    tokens, length = residual.shape[0], queries.shape[0]
    bf16, f32 = jnp.bfloat16, jnp.float32
    vmem, hbm = pl.BlockSpec(memory_space=pltpu.VMEM), pl.BlockSpec(memory_space=pl.ANY)
    dma = pltpu.SemaphoreType.DMA
    return pl.pallas_call(
        attention_kernel,
        out_shape=(
            jax.ShapeDtypeStruct((tokens, QUERY_HEADS * HEAD_SIZE), bf16),
            jax.ShapeDtypeStruct((tokens, KEY_VALUE_HEADS * HEAD_SIZE), bf16),
            jax.ShapeDtypeStruct((tokens, KEY_VALUE_HEADS * HEAD_SIZE), bf16),
        ),
        in_specs=[vmem] + [hbm] * 4,
        out_specs=(hbm, vmem, vmem),
        scratch_shapes=[
            pltpu.VMEM((length, D), bf16),
            pltpu.VMEM(w_out.shape, bf16),
            pltpu.VMEM(queries.shape, bf16),
            pltpu.VMEM(keys.shape, bf16),
            pltpu.VMEM(values.shape, bf16),
            pltpu.VMEM((length, 512), bf16),
            pltpu.VMEM((HEAD_SIZE, length), bf16),
            pltpu.VMEM((length, HEAD_SIZE), f32),
            pltpu.VMEM((length, HEAD_SIZE), f32),
            pltpu.VMEM((length, 768), bf16),
            pltpu.VMEM((8, tokens, 256), bf16),
            pltpu.VMEM((4, 256, 256), f32),
            pltpu.VMEM((4, 512, 256), f32),
            pltpu.VMEM((4, 768, 256), f32),
            pltpu.VMEM((4, 1024, 256), f32),
            dma((4,)),
            dma((13,)),
            dma((13,)),
            dma((8,)),
            dma((8,)),
            dma((8,)),
            dma((8,)),
        ],
        compiler_params=pltpu.CompilerParams(
            collective_id=2, has_side_effects=True, vmem_limit_bytes=56 << 20
        ),
        cost_estimate=pl.CostEstimate(
            flops=9_000_000_000, bytes_accessed=10_000_000, transcendentals=3_000_000
        ),
        name="attention_core",
    )(residual, w_out, queries, keys, values)


ORDER = 101
GROUP = 32
GROUPS = 4
ROWS = GROUP * 8
PART = ROWS + GROUP
TAIL = D // 8
WIDE = D + FFE
MESSAGE = WIDE + TAIL + HEAD_SIZE


def place_of(order, sign, here):
    x, c, y, z = here
    code = lax.rem(order * ORDER, 128)
    dc, dx, dy, dz = lax.rem(code, 2), lax.rem(code // 2, 4), lax.rem(code // 8, 4), code // 32
    if sign < 0:
        dx, dy, dz = 4 - dx, 4 - dy, 4 - dz
    return (
        lax.rem(x + dx, 4) * 2 + lax.rem(c + dc, 2),
        lax.rem(y + dy, 4) * 4 + lax.rem(z + dz, 4),
    )


def expert_of(order, here):
    seq, expert = place_of(order, 1, here)
    return seq * 16 + expert


def expert_kernel(
    state_ref, gain_ref, layer_ref, grads_ref, routes_ref, gate_hbm, up_hbm, query_hbm, key_hbm,
    value_hbm, residual_ref, gate_out, up_out, query_all, key_all, value_all,
    send, recv, back, back_recv, weights, rows_in, parts, stage, expert_in, hot, hot_t, last,
    codes, last_rows, weight_sem, send_sem, recv_sem, back_sem, back_recv_sem, out_sem,
    head_send, head_recv,
):
    seq, expert = lax.axis_index("seq"), lax.axis_index("expert")
    here = (seq // 2, lax.rem(seq, 2), expert // 4, lax.rem(expert, 4))
    turn = seq * 13 + expert * 7
    tokens = state_ref.shape[0]
    bf16, f32 = jnp.bfloat16, jnp.float32

    def iota(shape, axis):
        return lax.broadcasted_iota(jnp.int32, shape, axis)

    barrier = pltpu.get_barrier_semaphore()

    def greet(order, carry):
        pl.semaphore_signal(barrier, inc=1, device_id=place_of(order, 1, here), device_id_type=MESH)
        return carry

    lax.fori_loop(1, 128, greet, 0)
    gate_copy = pltpu.make_async_copy(gate_hbm, weights.at[:, pl.ds(0, FFE)], weight_sem.at[0])
    up_copy = pltpu.make_async_copy(up_hbm, weights.at[:, pl.ds(FFE, FFE)], weight_sem.at[1])
    gate_copy.start()
    up_copy.start()

    gain = gain_ref[...].astype(f32)
    gain = jnp.concatenate([gain[j : j + 1, :] for j in range(D // 128)], axis=1)
    state = state_ref[...].astype(f32)
    rstd = lax.rsqrt(jnp.mean(state * state, axis=-1, keepdims=True) + 1e-06)
    expert_in[...] = (state * rstd * gain).astype(bf16)

    pl.semaphore_wait(barrier, 127)

    def head_copies(step):
        dx, dc = step // 2, lax.rem(step, 2)
        to = lax.rem(here[0] + dx, 4) * 2 + lax.rem(here[1] + dc, 2)
        rows = pl.ds(pl.multiple_of(seq * tokens, tokens), tokens)
        wide = pl.ds(pl.multiple_of(to * 512, 512), 512)
        narrow = pl.ds(pl.multiple_of(to // 2 * HEAD_SIZE, HEAD_SIZE), HEAD_SIZE)
        return to, (
            (query_hbm.at[:, wide], query_all.at[rows, :]),
            (key_hbm.at[:, narrow], key_all.at[rows, :]),
            (value_hbm.at[:, narrow], value_all.at[rows, :]),
        )

    def head_remote(step):
        to, pairs = head_copies(step)
        return [
            pltpu.make_async_remote_copy(
                src_ref=source, dst_ref=target_ref, send_sem=head_send.at[n, step],
                recv_sem=head_recv.at[n, step], device_id=(to, expert), device_id_type=MESH,
            )
            for n, (source, target_ref) in enumerate(pairs)
        ]

    own = [
        pltpu.make_async_copy(source, target_ref, head_send.at[n, 0])
        for n, (source, target_ref) in enumerate(head_copies(0)[1])
    ]
    for copy in own:
        copy.start()

    def send_heads(step, carry):
        for copy in head_remote(step):
            copy.start()
        return carry

    lax.fori_loop(1, 8, send_heads, 0)

    lanes = iota((tokens, 128), 1)
    route = routes_ref[...].astype(f32).T
    named = [route[:, k : k + 1] == lanes.astype(f32) for k in range(TOP)]
    count = sum(jnp.where(n, 1.0, 0.0) for n in named)
    earlier = jnp.where(iota((tokens, tokens), 0) > iota((tokens, tokens), 1), 1.0, 0.0)
    rank = dot(earlier.astype(bf16), count.astype(bf16), NN)
    columns = iota((tokens, tokens * TOP), 1) - iota((tokens, tokens * TOP), 0) * TOP
    spread_codes = jnp.zeros((tokens, tokens * TOP), f32)
    for k in range(TOP):
        route_rank = jnp.sum(jnp.where(named[k], rank, 0.0), axis=1, keepdims=True)
        code = route[:, k : k + 1] * 16.0 + route_rank
        spread_codes = jnp.where(columns == k, code, spread_codes)
    codes[...] = jnp.sum(spread_codes, axis=0, keepdims=True)
    target = expert_of(iota((128, 128), 0), here)
    ordered = jnp.where(target == iota((128, 128), 1), 1.0, 0.0).astype(bf16)
    rank_t = dot(ordered, jnp.where(count > 0.0, rank, -1.0).astype(bf16), NT)
    slot = iota((128, 8, tokens), 1).astype(f32)
    rank_wide = jnp.broadcast_to(rank_t[:, None, :], (128, 8, tokens))
    hot_full = jnp.where(rank_wide == slot, 1.0, 0.0).reshape(1024, tokens)
    hot[...] = hot_full.astype(bf16)
    hot_t[:, 0:1024] = hot_full.T.astype(bf16)
    last_full = jnp.where(rank_wide == 8.0, 1.0, 0.0).reshape(1024, tokens)
    hot_t[:, 1024:2048] = last_full.T.astype(bf16)
    last[...] = jnp.where(rank_t == 8.0, 1.0, 0.0).astype(bf16)

    row, col = iota((ROWS, ROWS), 0), iota((ROWS, ROWS), 1)
    spread = jnp.where(col == lax.rem(row, 8) * GROUP + row // 8, 1.0, 0.0).astype(bf16)
    gather = jnp.where(row == lax.rem(col, 8) * GROUP + col // 8, 1.0, 0.0).astype(bf16)

    def dispatch(g, carry):
        at = pl.ds(g * GROUP, GROUP)
        rows = pl.ds(pl.multiple_of(g * ROWS, ROWS), ROWS)
        first = g * GROUP
        x_rows = dot(hot[rows, :], expert_in[...], NN).astype(bf16)
        send[at, :, 0:D] = x_rows.reshape(GROUP, 8, D)
        number = iota((ROWS, 128), 0)
        row_code = (expert_of(first + number // 8, here) * 16 + lax.rem(number, 8)).astype(f32)
        last_code = (expert_of(first + iota((GROUP, 128), 0), here) * 16 + 8).astype(f32)

        def one_hot(code):
            pieces = [
                jnp.where(codes[:, j * 128 : (j + 1) * 128] == code, 1.0, 0.0).astype(bf16)
                for j in range(TOP)
            ]
            return jnp.concatenate(pieces, axis=1)

        h_rows = dot(one_hot(row_code), grads_ref[...], NN).astype(bf16)
        send[at, :, D:WIDE] = h_rows.reshape(GROUP, 8, FFE)
        x_last = dot(last[pl.ds(pl.multiple_of(first, GROUP), GROUP), :], expert_in[...], NN)
        x_last = x_last.astype(bf16)
        h_last = dot(one_hot(last_code), grads_ref[...], NN).astype(bf16)
        x_stack = jnp.concatenate([x_last[:, s * TAIL : (s + 1) * TAIL] for s in range(8)], axis=0)
        h_stack = jnp.concatenate([h_last[:, s * 128 : (s + 1) * 128] for s in range(6)], axis=0)
        x_tail = dot(spread, x_stack, NN).astype(bf16)
        h_tail = dot(spread[:, 0 : 6 * GROUP], h_stack, NN).astype(bf16)
        send[at, :, WIDE : WIDE + TAIL] = x_tail.reshape(GROUP, 8, TAIL)
        send[at, :, WIDE + TAIL : MESSAGE] = h_tail.reshape(GROUP, 8, HEAD_SIZE)

        def start(step, inner):
            order = first + lax.rem(step + turn, GROUP)
            copy = pltpu.make_async_remote_copy(
                src_ref=send.at[order], dst_ref=recv.at[order], send_sem=send_sem,
                recv_sem=recv_sem.at[g], device_id=place_of(order, 1, here), device_id_type=MESH,
            )
            pl.when(order > 0)(copy.start)
            return inner

        lax.fori_loop(0, GROUP, start, 0)
        return carry

    lax.fori_loop(0, GROUPS, dispatch, 0)
    pltpu.make_async_copy(send.at[0], recv.at[0], recv_sem.at[0]).start()
    gate_copy.wait()
    up_copy.wait()

    def work(g, carry):
        at = pl.ds(g * GROUP, GROUP)
        first = g * GROUP
        whole = pl.ds(pl.multiple_of(g * PART, GROUP), PART)
        main = pl.ds(pl.multiple_of(g * PART, GROUP), ROWS)
        tail = pl.ds(pl.multiple_of(g * PART + ROWS, GROUP), GROUP)
        pltpu.make_async_copy(recv.at[at], recv.at[at], recv_sem.at[g]).wait()
        rows_in[main, :] = recv[at, :, 0:D].reshape(ROWS, D)
        x_last = dot(gather, recv[at, :, WIDE : WIDE + TAIL].reshape(ROWS, TAIL), NN).astype(bf16)
        for s in range(8):
            rows_in[tail, s * TAIL : (s + 1) * TAIL] = x_last[s * GROUP : (s + 1) * GROUP, :]
        h_last = dot(
            gather, recv[at, :, WIDE + TAIL : MESSAGE].reshape(ROWS, HEAD_SIZE), NN
        )
        h_last = jnp.concatenate([h_last[s * GROUP : (s + 1) * GROUP, :] for s in range(6)], axis=1)
        for n in range(3):
            tile = slice(n * 256, (n + 1) * 256)
            shifted = slice(FFE + n * 256, FFE + (n + 1) * 256)
            rows_grad = jnp.concatenate(
                [
                    recv[at, :, D + n * 256 : D + (n + 1) * 256].reshape(ROWS, 256).astype(f32),
                    h_last[:, tile],
                ],
                axis=0,
            )
            gate_pre = dot(rows_in[whole, :], weights[:, tile], NN)
            up_pre = dot(rows_in[whole, :], weights[:, shifted], NN)
            sig = jax.nn.sigmoid(gate_pre)
            gate_part = rows_grad * up_pre * sig * (1.0 + gate_pre * (1.0 - sig))
            parts[whole, tile] = gate_part.astype(bf16)
            parts[whole, shifted] = (rows_grad * gate_pre * sig).astype(bf16)

        def back_tile(n, inner):
            source = pl.ds(pl.multiple_of(n * 256, 256), 256)
            rows_back = dot(parts[whole, :], weights[source, :], NT).astype(bf16)
            back[at, :, source] = rows_back[:ROWS, :].reshape(GROUP, 8, 256)
            last_rows[pl.ds(pl.multiple_of(n * GROUP, GROUP), GROUP), :] = rows_back[ROWS:, :]
            return inner

        lax.fori_loop(0, 8, back_tile, 0)
        tails = dot(spread, last_rows[...], NN).astype(bf16)
        back[at, :, D : D + TAIL] = tails.reshape(GROUP, 8, TAIL)

        def start(step, inner):
            order = first + lax.rem(step + turn, GROUP)
            copy = pltpu.make_async_remote_copy(
                src_ref=back.at[order], dst_ref=back_recv.at[order], send_sem=back_sem,
                recv_sem=back_recv_sem, device_id=place_of(order, -1, here), device_id_type=MESH,
            )
            pl.when(order > 0)(copy.start)
            return inner

        lax.fori_loop(0, GROUP, start, 0)
        return carry

    lax.fori_loop(0, GROUPS, work, 0)
    pltpu.make_async_copy(back.at[0], back_recv.at[0], back_recv_sem).start()

    def weight_grads(f, carry):
        tile = pl.ds(pl.multiple_of(f * 256, 256), 256)
        stage[tile, :] = dot(rows_in[:, tile], parts[...], TN).astype(bf16)
        pltpu.make_async_copy(
            stage.at[tile, pl.ds(0, FFE)], gate_out.at[tile, :], out_sem.at[0]
        ).start()
        pltpu.make_async_copy(
            stage.at[tile, pl.ds(FFE, FFE)], up_out.at[tile, :], out_sem.at[1]
        ).start()
        return carry

    lax.fori_loop(0, 8, weight_grads, 0)

    pltpu.make_async_copy(back_recv, back_recv, back_recv_sem).wait()
    slot_of = lax.rem(iota((tokens, 1024), 1), 8)
    state = state_ref[...].astype(f32)
    rstd = lax.rsqrt(jnp.mean(state * state, axis=-1, keepdims=True) + 1e-06)
    inner = jnp.zeros((tokens, 1), f32)
    weighted = []
    for n in range(8):
        tile = slice(n * 256, (n + 1) * 256)
        routed = dot(hot_t[:, 0:1024], back_recv[:, :, tile].reshape(1024, 256), NN)
        chosen = jnp.where(slot_of == n, hot_t[:, 1024:2048], jnp.zeros((), bf16))
        routed += dot(chosen, back_recv[:, :, D : D + TAIL].reshape(1024, TAIL), NN)
        weighted.append(gain[:, tile] * routed)
        inner += jnp.sum(weighted[n] * (state[:, tile] * rstd), axis=-1, keepdims=True)
    inner = inner * (1.0 / D)
    for n in range(8):
        tile = slice(n * 256, (n + 1) * 256)
        change = rstd * (weighted[n] - state[:, tile] * rstd * inner)
        residual_ref[:, tile] = (layer_ref[:, tile].astype(f32) + change).astype(bf16)

    pltpu.make_async_copy(stage.at[:, pl.ds(0, FFE)], gate_out, out_sem.at[0]).wait()
    pltpu.make_async_copy(stage.at[:, pl.ds(FFE, FFE)], up_out, out_sem.at[1]).wait()
    pltpu.make_async_copy(
        send.at[pl.ds(1, 127)], recv.at[pl.ds(1, 127)], send_sem
    ).wait()
    pltpu.make_async_copy(
        back.at[pl.ds(1, 127)], back_recv.at[pl.ds(1, 127)], back_sem
    ).wait()
    for copy in own:
        copy.wait()

    def finish_heads(step, carry):
        for copy in head_remote(step):
            copy.wait()
        return carry

    lax.fori_loop(1, 8, finish_heads, 0)


def expert_block(state, gain, layer_grad, grads, routes, w_gate, w_up, queries, keys, values):
    tokens = state.shape[0]
    bf16, f32 = jnp.bfloat16, jnp.float32
    vmem, hbm = pl.BlockSpec(memory_space=pltpu.VMEM), pl.BlockSpec(memory_space=pl.ANY)
    length = tokens * lax.axis_size("seq")
    dma = pltpu.SemaphoreType.DMA
    return pl.pallas_call(
        expert_kernel,
        out_shape=(
            jax.ShapeDtypeStruct((tokens, D), bf16),
            jax.ShapeDtypeStruct(w_gate.shape, bf16),
            jax.ShapeDtypeStruct(w_up.shape, bf16),
            jax.ShapeDtypeStruct((length, 512), bf16),
            jax.ShapeDtypeStruct((length, HEAD_SIZE), bf16),
            jax.ShapeDtypeStruct((length, HEAD_SIZE), bf16),
        ),
        in_specs=[vmem] * 5 + [hbm] * 5,
        out_specs=(vmem,) + (hbm,) * 5,
        scratch_shapes=[
            pltpu.VMEM((128, 8, MESSAGE), bf16),
            pltpu.VMEM((128, 8, MESSAGE), bf16),
            pltpu.VMEM((128, 8, D + TAIL), bf16),
            pltpu.VMEM((128, 8, D + TAIL), bf16),
            pltpu.VMEM((D, 2 * FFE), bf16),
            pltpu.VMEM((GROUPS * PART, D), bf16),
            pltpu.VMEM((GROUPS * PART, 2 * FFE), bf16),
            pltpu.VMEM((D, 2 * FFE), bf16),
            pltpu.VMEM((tokens, D), bf16),
            pltpu.VMEM((1024, tokens), bf16),
            pltpu.VMEM((tokens, 2048), bf16),
            pltpu.VMEM((128, tokens), bf16),
            pltpu.VMEM((1, tokens * TOP), f32),
            pltpu.VMEM((ROWS, TAIL), bf16),
            dma((2,)),
            dma,
            dma((GROUPS,)),
            dma,
            dma,
            dma((2,)),
            dma((3, 8)),
            dma((3, 8)),
        ],
        compiler_params=pltpu.CompilerParams(
            collective_id=1, has_side_effects=True, vmem_limit_bytes=60 << 20
        ),
        cost_estimate=pl.CostEstimate(
            flops=30_000_000_000, bytes_accessed=20_000_000, transcendentals=1_000_000
        ),
        name="expert_block",
    )(state, gain, layer_grad, grads, routes, w_gate, w_up, queries, keys, values)


def finish_kernel(count, *refs):
    sources, targets, sems = refs[:count], refs[count : 2 * count], refs[2 * count]
    copies = [
        pltpu.make_async_copy(sources[n], targets[n], sems.at[n]) for n in range(count)
    ]
    for copy in copies:
        copy.start()
    for copy in copies:
        copy.wait()


def finish(*arrays):
    hbm = pl.BlockSpec(memory_space=pl.ANY)
    return pl.pallas_call(
        functools.partial(finish_kernel, len(arrays)),
        out_shape=tuple(jax.ShapeDtypeStruct(a.shape, a.dtype) for a in arrays),
        in_specs=[hbm] * len(arrays),
        out_specs=(hbm,) * len(arrays),
        scratch_shapes=[pltpu.SemaphoreType.DMA((len(arrays),))],
        compiler_params=pltpu.CompilerParams(vmem_limit_bytes=1 << 20),
        name="finish",
    )(*arrays)


def local(
    queries,
    keys,
    values,
    w_out,
    hidden_state,
    norm_gain,
    layer_grad,
    hidden_grad,
    routes,
    w_gate,
    w_up,
):
    residual_rows, gate_grad, up_grad, query_all, key_all, value_all = expert_block(
        hidden_state[0],
        norm_gain.reshape(D // 128, 128),
        layer_grad[0],
        hidden_grad[0].reshape(-1, FFE),
        routes[0].T,
        w_gate[0],
        w_up[0],
        queries[0],
        keys[0],
        values[0],
    )
    query_out, key_out, value_out = attention_core(
        residual_rows, w_out, query_all, key_all, value_all
    )
    outs = (query_out, key_out, value_out, residual_rows, gate_grad, up_grad)
    return tuple(out[None] for out in finish(*outs))


def solution(mesh):
    return jax.shard_map(
        local,
        mesh=mesh,
        in_specs=(
            P("expert", "seq", None),
            P("expert", "seq", None),
            P("expert", "seq", None),
            P("seq", None),
            P("expert", "seq", None),
            P(),
            P("expert", "seq", None),
            P("expert", "seq", None, None),
            P("expert", "seq", None),
            P(("seq", "expert"), None, None),
            P(("seq", "expert"), None, None),
        ),
        out_specs=(
            P("expert", "seq", None),
            P("expert", "seq", None),
            P("expert", "seq", None),
            P("expert", "seq", None),
            P(("seq", "expert"), None, None),
            P(("seq", "expert"), None, None),
        ),
        check_vma=False,
    )
```

```python
import functools

import jax
import jax.numpy as jnp
from jax import lax
from jax.experimental import pallas as pl
from jax.experimental.pallas import tpu as pltpu
from jax.sharding import PartitionSpec as P

D = 2048
QUERY_HEADS = 32
KEY_VALUE_HEADS = 4
HEAD_SIZE = 128
FFE = 768
TOP = 8
LOG2E = 1.4426950408889634

NN = (((1,), (0,)), ((), ()))
NT = (((1,), (1,)), ((), ()))
TN = (((0,), (0,)), ((), ()))
MESH = pl.DeviceIdType.MESH


def dot(a, b, dims):
    return lax.dot_general(a, b, dims, preferred_element_type=jnp.float32)


def attention_kernel(
    residual_ref, w_hbm, query_hbm, key_hbm, value_hbm, query_out, key_out, value_out,
    gathered, w_out, queries, keys, values, grad, key_t, dk, dv, packed, returned,
    probs_0, probs_1, probs_2, probs_3, load_sem, gather_send, gather_recv,
    query_send, query_recv, pair_send, pair_recv,
):
    seq, expert = lax.axis_index("seq"), lax.axis_index("expert")
    x, c = seq // 2, lax.rem(seq, 2)
    tokens = residual_ref.shape[0]
    half = tokens // 2
    bf16, f32 = jnp.bfloat16, jnp.float32
    factor = HEAD_SIZE ** (-0.5)
    probs = (probs_0, probs_1, probs_2, probs_3)
    block = 2 * tokens

    def device(dx, dc):
        return lax.rem(x + dx, 4) * 2 + lax.rem(c + dc, 2)

    barrier = pltpu.get_barrier_semaphore()
    for step in range(1, 8):
        pl.semaphore_signal(
            barrier, inc=1, device_id=(device(step // 2, step % 2), expert), device_id_type=MESH
        )
    loads = [
        pltpu.make_async_copy(source, target, load_sem.at[n])
        for n, (source, target) in enumerate(
            ((query_hbm, queries), (key_hbm, keys), (value_hbm, values), (w_hbm, w_out))
        )
    ]
    for load in loads:
        load.start()

    def rows_of(owner, start, size):
        return pl.ds(pl.multiple_of(owner * tokens + start, size), size)

    def gather_copy(number, owner, start, size, to):
        rows = rows_of(owner, start, size)
        return pltpu.make_async_remote_copy(
            src_ref=gathered.at[rows, :], dst_ref=gathered.at[rows, :],
            send_sem=gather_send.at[number], recv_sem=gather_recv.at[number],
            device_id=(to, expert), device_id_type=MESH,
        )

    own, left, right, far = device(0, 0), device(3, 0), device(1, 0), device(2, 0)
    mate = device(0, 1)
    gathered[rows_of(own, 0, tokens), :] = residual_ref[...]
    pl.semaphore_wait(barrier, 7)
    copies = [
        gather_copy(0, own, 0, half, right),
        gather_copy(1, own, half, half, left),
        gather_copy(2, own, half, half, right),
        gather_copy(3, own, 0, half, left),
        gather_copy(4, own, 0, tokens, mate),
        gather_copy(5, left, 0, half, right),
        gather_copy(6, right, half, half, left),
        gather_copy(7, left, 0, half, mate),
        gather_copy(8, right, half, half, mate),
        gather_copy(9, left, half, half, mate),
        gather_copy(10, right, 0, half, mate),
        gather_copy(11, far, 0, half, mate),
        gather_copy(12, far, half, half, mate),
    ]
    for copy in copies[:5]:
        copy.start()
    for load in loads:
        load.wait()

    key_t[...] = keys[...].astype(f32).T.astype(bf16)
    dk[...] = jnp.zeros_like(dk)
    dv[...] = jnp.zeros_like(dv)

    def softmax_block(i):
        lower, upper = i * block, (i + 1) * block
        key_pos = lax.broadcasted_iota(jnp.int32, (block, block), 0)
        query_pos = lax.broadcasted_iota(jnp.int32, (block, block), 1)
        for head in range(4):
            columns = slice(head * HEAD_SIZE, (head + 1) * HEAD_SIZE)
            scores = dot(keys[0:upper, :], queries[lower:upper, columns], NT) * (factor * LOG2E)
            diagonal = jnp.where(key_pos <= query_pos, scores[lower:upper], -1e30)
            scores = diagonal if i == 0 else jnp.concatenate([scores[:lower], diagonal], axis=0)
            exps = jnp.exp2(scores - jnp.max(scores, axis=0, keepdims=True))
            probs[i][head, :, :] = exps * (1.0 / jnp.sum(exps, axis=0, keepdims=True))

    def project(owner):
        rows = rows_of(owner, 0, tokens)
        grad[rows, :] = dot(gathered[rows, :], w_out[...], NT).astype(bf16)

    softmax_block(0)
    softmax_block(1)
    copies[0].wait_recv()
    copies[5].start()
    copies[7].start()
    copies[1].wait_recv()
    copies[6].start()
    copies[8].start()
    softmax_block(2)
    copies[2].wait_recv()
    copies[9].start()
    copies[3].wait_recv()
    copies[10].start()
    softmax_block(3)
    project(own)
    copies[4].wait_recv()
    project(mate)
    project(left)
    project(right)
    copies[5].wait_recv()
    copies[11].start()
    copies[6].wait_recv()
    copies[12].start()
    project(far)
    for copy in copies[7:11]:
        copy.wait_recv()
    project(device(3, 1))
    project(device(1, 1))
    for copy in copies[11:]:
        copy.wait_recv()
    project(device(2, 1))

    def backward_block(i):
        lower, upper = i * block, (i + 1) * block
        for head in range(4):
            columns = slice(head * HEAD_SIZE, (head + 1) * HEAD_SIZE)
            out_grad = grad[lower:upper, columns]
            prob = probs[i][head]
            dv[0:upper, :] += dot(prob.astype(bf16), out_grad, NN)
            prob_grad = dot(values[0:upper, :], out_grad, NT)
            delta = jnp.sum(prob * prob_grad, axis=0, keepdims=True)
            score_grad = (prob * (prob_grad - delta)).astype(bf16)
            dk[0:upper, :] += dot(score_grad, queries[lower:upper, columns], NN)
            query_grad = dot(key_t[:, 0:upper], score_grad, NN) * factor
            packed[lower:upper, columns] = query_grad.T.astype(bf16)

    pair = slice(4 * HEAD_SIZE, 6 * HEAD_SIZE)

    def query_copy(dx, dc):
        to, number = device(dx, dc), dx * 2 + dc
        return pltpu.make_async_remote_copy(
            src_ref=packed.at[rows_of(to, 0, tokens), pl.ds(0, 512)],
            dst_ref=query_out.at[:, pl.ds(pl.multiple_of(seq * 512, 512), 512)],
            send_sem=query_send.at[number], recv_sem=query_recv.at[number],
            device_id=(to, expert), device_id_type=MESH,
        )

    def pair_copy(dx, dc):
        to, number = device(dx, dc), dx * 2 + dc
        return pltpu.make_async_remote_copy(
            src_ref=packed.at[rows_of(to, 0, tokens), pl.ds(512, 256)],
            dst_ref=returned.at[seq],
            send_sem=pair_send.at[number], recv_sem=pair_recv.at[number],
            device_id=(to, expert), device_id_type=MESH,
        )

    own_query = pltpu.make_async_copy(
        packed.at[rows_of(seq, 0, tokens), pl.ds(0, 512)],
        query_out.at[:, pl.ds(pl.multiple_of(seq * 512, 512), 512)],
        query_send.at[0],
    )

    def backward_step(step, carry):
        dx = lax.rem(step + 1, 4)
        chip = lax.rem(x + dx, 4)
        for i in range(4):
            pl.when(chip == i)(functools.partial(backward_block, i))

        @pl.when(step < 3)
        def _():
            query_copy(dx, 0).start()

        @pl.when(step == 3)
        def _():
            own_query.start()

        query_copy(dx, 1).start()
        return carry

    lax.fori_loop(0, 4, backward_step, 0)
    packed[:, 512:640] = (dk[...] * factor).astype(bf16)
    packed[:, 640:768] = dv[...].astype(bf16)
    for step in (2, 3, 4, 5, 6, 7, 1):
        pair_copy(step // 2, step % 2).start()
    returned[seq, :, :] = packed[rows_of(seq, 0, tokens), pair]
    for step in range(1, 8):
        pair_copy(step // 2, step % 2).wait_recv()
    for head in range(KEY_VALUE_HEADS):
        total = returned[2 * head].astype(f32) + returned[2 * head + 1].astype(f32)
        columns = slice(head * HEAD_SIZE, (head + 1) * HEAD_SIZE)
        key_out[:, columns] = total[:, 0:HEAD_SIZE].astype(bf16)
        value_out[:, columns] = total[:, HEAD_SIZE:].astype(bf16)
    for copy in copies:
        copy.wait_send()
    for step in range(1, 8):
        query_copy(step // 2, step % 2).wait()
        pair_copy(step // 2, step % 2).wait_send()
    own_query.wait()


def attention_core(residual, w_out, queries, keys, values):
    tokens, length = residual.shape[0], queries.shape[0]
    bf16, f32 = jnp.bfloat16, jnp.float32
    vmem, hbm = pl.BlockSpec(memory_space=pltpu.VMEM), pl.BlockSpec(memory_space=pl.ANY)
    dma = pltpu.SemaphoreType.DMA
    return pl.pallas_call(
        attention_kernel,
        out_shape=(
            jax.ShapeDtypeStruct((tokens, QUERY_HEADS * HEAD_SIZE), bf16),
            jax.ShapeDtypeStruct((tokens, KEY_VALUE_HEADS * HEAD_SIZE), bf16),
            jax.ShapeDtypeStruct((tokens, KEY_VALUE_HEADS * HEAD_SIZE), bf16),
        ),
        in_specs=[vmem] + [hbm] * 4,
        out_specs=(hbm, vmem, vmem),
        scratch_shapes=[
            pltpu.VMEM((length, D), bf16),
            pltpu.VMEM(w_out.shape, bf16),
            pltpu.VMEM(queries.shape, bf16),
            pltpu.VMEM(keys.shape, bf16),
            pltpu.VMEM(values.shape, bf16),
            pltpu.VMEM((length, 512), bf16),
            pltpu.VMEM((HEAD_SIZE, length), bf16),
            pltpu.VMEM((length, HEAD_SIZE), f32),
            pltpu.VMEM((length, HEAD_SIZE), f32),
            pltpu.VMEM((length, 768), bf16),
            pltpu.VMEM((8, tokens, 256), bf16),
            pltpu.VMEM((4, 256, 256), f32),
            pltpu.VMEM((4, 512, 256), f32),
            pltpu.VMEM((4, 768, 256), f32),
            pltpu.VMEM((4, 1024, 256), f32),
            dma((4,)),
            dma((13,)),
            dma((13,)),
            dma((8,)),
            dma((8,)),
            dma((8,)),
            dma((8,)),
        ],
        compiler_params=pltpu.CompilerParams(
            collective_id=2, has_side_effects=True, vmem_limit_bytes=56 << 20
        ),
        cost_estimate=pl.CostEstimate(
            flops=9_000_000_000, bytes_accessed=10_000_000, transcendentals=3_000_000
        ),
        name="attention_core",
    )(residual, w_out, queries, keys, values)


ORDER = 101
GROUP = 32
GROUPS = 4
ROWS = GROUP * 8
PART = ROWS + GROUP
TAIL = D // 8
WIDE = D + FFE
MESSAGE = WIDE + TAIL + HEAD_SIZE


def place_of(order, sign, here):
    x, c, y, z = here
    code = lax.rem(order * ORDER, 128)
    dc, dx, dy, dz = lax.rem(code, 2), lax.rem(code // 2, 4), lax.rem(code // 8, 4), code // 32
    if sign < 0:
        dx, dy, dz = 4 - dx, 4 - dy, 4 - dz
    return (
        lax.rem(x + dx, 4) * 2 + lax.rem(c + dc, 2),
        lax.rem(y + dy, 4) * 4 + lax.rem(z + dz, 4),
    )


def expert_of(order, here):
    seq, expert = place_of(order, 1, here)
    return seq * 16 + expert


def expert_kernel(
    state_ref, gain_ref, layer_ref, grads_ref, routes_ref, gate_hbm, up_hbm, query_hbm, key_hbm,
    value_hbm, residual_ref, gate_out, up_out, query_all, key_all, value_all,
    send, recv, back, back_recv, weights, rows_in, parts, stage, expert_in, hot, hot_t, last,
    codes, last_rows, total, weight_sem, send_sem, recv_sem, back_sem, back_recv_sem, out_sem,
    head_send, head_recv,
):
    seq, expert = lax.axis_index("seq"), lax.axis_index("expert")
    here = (seq // 2, lax.rem(seq, 2), expert // 4, lax.rem(expert, 4))
    turn = seq * 13 + expert * 7
    tokens = state_ref.shape[0]
    bf16, f32 = jnp.bfloat16, jnp.float32

    def iota(shape, axis):
        return lax.broadcasted_iota(jnp.int32, shape, axis)

    barrier = pltpu.get_barrier_semaphore()

    def greet(order, carry):
        pl.semaphore_signal(barrier, inc=1, device_id=place_of(order, 1, here), device_id_type=MESH)
        return carry

    lax.fori_loop(1, 128, greet, 0)
    gate_copy = pltpu.make_async_copy(gate_hbm, weights.at[:, pl.ds(0, FFE)], weight_sem.at[0])
    up_copy = pltpu.make_async_copy(up_hbm, weights.at[:, pl.ds(FFE, FFE)], weight_sem.at[1])
    gate_copy.start()
    up_copy.start()

    gain = gain_ref[...].astype(f32)
    gain = jnp.concatenate([gain[j : j + 1, :] for j in range(D // 128)], axis=1)
    state = state_ref[...].astype(f32)
    rstd = lax.rsqrt(jnp.mean(state * state, axis=-1, keepdims=True) + 1e-06)
    expert_in[...] = (state * rstd * gain).astype(bf16)

    pl.semaphore_wait(barrier, 127)

    def head_copies(step):
        dx, dc = step // 2, lax.rem(step, 2)
        to = lax.rem(here[0] + dx, 4) * 2 + lax.rem(here[1] + dc, 2)
        rows = pl.ds(pl.multiple_of(seq * tokens, tokens), tokens)
        wide = pl.ds(pl.multiple_of(to * 512, 512), 512)
        narrow = pl.ds(pl.multiple_of(to // 2 * HEAD_SIZE, HEAD_SIZE), HEAD_SIZE)
        return to, (
            (query_hbm.at[:, wide], query_all.at[rows, :]),
            (key_hbm.at[:, narrow], key_all.at[rows, :]),
            (value_hbm.at[:, narrow], value_all.at[rows, :]),
        )

    def head_remote(step):
        to, pairs = head_copies(step)
        return [
            pltpu.make_async_remote_copy(
                src_ref=source, dst_ref=target_ref, send_sem=head_send.at[n, step],
                recv_sem=head_recv.at[n, step], device_id=(to, expert), device_id_type=MESH,
            )
            for n, (source, target_ref) in enumerate(pairs)
        ]

    own = [
        pltpu.make_async_copy(source, target_ref, head_send.at[n, 0])
        for n, (source, target_ref) in enumerate(head_copies(0)[1])
    ]
    for copy in own:
        copy.start()

    for step in (2, 6, 4, 1, 3, 5, 7):
        copies = head_remote(step)
        for copy in copies if step in (1, 2, 4, 6) else copies[:1]:
            copy.start()

    def hand_on(dx):
        rows = pl.ds(
            pl.multiple_of((lax.rem(here[0] + 4 - dx, 4) * 2 + here[1]) * tokens, tokens), tokens
        )
        mate = here[0] * 2 + 1 - here[1]
        return [
            pltpu.make_async_remote_copy(
                src_ref=array.at[rows, :], dst_ref=array.at[rows, :],
                send_sem=head_send.at[n, 2 * dx + 1], recv_sem=head_recv.at[n, 2 * dx + 1],
                device_id=(mate, expert), device_id_type=MESH,
            )
            for n, array in ((1, key_all), (2, value_all))
        ]


    lanes = iota((tokens, 128), 1)
    route = routes_ref[...].astype(f32).T
    named = [route[:, k : k + 1] == lanes.astype(f32) for k in range(TOP)]
    count = sum(jnp.where(n, 1.0, 0.0) for n in named)
    earlier = jnp.where(iota((tokens, tokens), 0) > iota((tokens, tokens), 1), 1.0, 0.0)
    rank = dot(earlier.astype(bf16), count.astype(bf16), NN)
    columns = iota((tokens, tokens * TOP), 1) - iota((tokens, tokens * TOP), 0) * TOP
    spread_codes = jnp.zeros((tokens, tokens * TOP), f32)
    for k in range(TOP):
        route_rank = jnp.sum(jnp.where(named[k], rank, 0.0), axis=1, keepdims=True)
        code = route[:, k : k + 1] * 16.0 + route_rank
        spread_codes = jnp.where(columns == k, code, spread_codes)
    codes[...] = jnp.sum(spread_codes, axis=0, keepdims=True)
    target = expert_of(iota((128, 128), 0), here)
    ordered = jnp.where(target == iota((128, 128), 1), 1.0, 0.0).astype(bf16)
    rank_t = dot(ordered, jnp.where(count > 0.0, rank, -1.0).astype(bf16), NT)
    slot = iota((128, 8, tokens), 1).astype(f32)
    rank_wide = jnp.broadcast_to(rank_t[:, None, :], (128, 8, tokens))
    hot_full = jnp.where(rank_wide == slot, 1.0, 0.0).reshape(1024, tokens)
    hot[...] = hot_full.astype(bf16)
    hot_t[:, 0:1024] = hot_full.T.astype(bf16)
    last_full = jnp.where(rank_wide == 8.0, 1.0, 0.0).reshape(1024, tokens)
    hot_t[:, 1024:2048] = last_full.T.astype(bf16)
    last[...] = jnp.where(rank_t == 8.0, 1.0, 0.0).astype(bf16)

    row, col = iota((ROWS, ROWS), 0), iota((ROWS, ROWS), 1)
    spread = jnp.where(col == lax.rem(row, 8) * GROUP + row // 8, 1.0, 0.0).astype(bf16)
    gather = jnp.where(row == lax.rem(col, 8) * GROUP + col // 8, 1.0, 0.0).astype(bf16)

    def dispatch(g, carry):
        at = pl.ds(g * GROUP, GROUP)
        rows = pl.ds(pl.multiple_of(g * ROWS, ROWS), ROWS)
        first = g * GROUP
        x_rows = dot(hot[rows, :], expert_in[...], NN).astype(bf16)
        send[at, :, 0:D] = x_rows.reshape(GROUP, 8, D)
        number = iota((ROWS, 128), 0)
        row_code = (expert_of(first + number // 8, here) * 16 + lax.rem(number, 8)).astype(f32)
        last_code = (expert_of(first + iota((GROUP, 128), 0), here) * 16 + 8).astype(f32)

        def one_hot(code):
            pieces = [
                jnp.where(codes[:, j * 128 : (j + 1) * 128] == code, 1.0, 0.0).astype(bf16)
                for j in range(TOP)
            ]
            return jnp.concatenate(pieces, axis=1)

        h_rows = dot(one_hot(row_code), grads_ref[...], NN).astype(bf16)
        send[at, :, D:WIDE] = h_rows.reshape(GROUP, 8, FFE)
        x_last = dot(last[pl.ds(pl.multiple_of(first, GROUP), GROUP), :], expert_in[...], NN)
        x_last = x_last.astype(bf16)
        h_last = dot(one_hot(last_code), grads_ref[...], NN).astype(bf16)
        x_stack = jnp.concatenate([x_last[:, s * TAIL : (s + 1) * TAIL] for s in range(8)], axis=0)
        h_stack = jnp.concatenate([h_last[:, s * 128 : (s + 1) * 128] for s in range(6)], axis=0)
        x_tail = dot(spread, x_stack, NN).astype(bf16)
        h_tail = dot(spread[:, 0 : 6 * GROUP], h_stack, NN).astype(bf16)
        send[at, :, WIDE : WIDE + TAIL] = x_tail.reshape(GROUP, 8, TAIL)
        send[at, :, WIDE + TAIL : MESSAGE] = h_tail.reshape(GROUP, 8, HEAD_SIZE)

        def start(step, inner):
            order = first + lax.rem(step + turn, GROUP)
            copy = pltpu.make_async_remote_copy(
                src_ref=send.at[order], dst_ref=recv.at[order], send_sem=send_sem,
                recv_sem=recv_sem.at[g], device_id=place_of(order, 1, here), device_id_type=MESH,
            )
            pl.when(order > 0)(copy.start)
            return inner

        lax.fori_loop(0, GROUP, start, 0)
        return carry

    lax.fori_loop(0, GROUPS, dispatch, 0)
    pltpu.make_async_copy(send.at[0], recv.at[0], recv_sem.at[0]).start()
    gate_copy.wait()
    up_copy.wait()

    def work(g, carry):
        at = pl.ds(g * GROUP, GROUP)
        first = g * GROUP
        whole = pl.ds(pl.multiple_of(g * PART, GROUP), PART)
        main = pl.ds(pl.multiple_of(g * PART, GROUP), ROWS)
        tail = pl.ds(pl.multiple_of(g * PART + ROWS, GROUP), GROUP)
        pltpu.make_async_copy(recv.at[at], recv.at[at], recv_sem.at[g]).wait()
        rows_in[main, :] = recv[at, :, 0:D].reshape(ROWS, D)
        x_last = dot(gather, recv[at, :, WIDE : WIDE + TAIL].reshape(ROWS, TAIL), NN).astype(bf16)
        for s in range(8):
            rows_in[tail, s * TAIL : (s + 1) * TAIL] = x_last[s * GROUP : (s + 1) * GROUP, :]
        h_last = dot(
            gather, recv[at, :, WIDE + TAIL : MESSAGE].reshape(ROWS, HEAD_SIZE), NN
        )
        h_last = jnp.concatenate([h_last[s * GROUP : (s + 1) * GROUP, :] for s in range(6)], axis=1)
        for n in range(3):
            tile = slice(n * 256, (n + 1) * 256)
            shifted = slice(FFE + n * 256, FFE + (n + 1) * 256)
            rows_grad = jnp.concatenate(
                [
                    recv[at, :, D + n * 256 : D + (n + 1) * 256].reshape(ROWS, 256).astype(f32),
                    h_last[:, tile],
                ],
                axis=0,
            )
            gate_pre = dot(rows_in[whole, :], weights[:, tile], NN)
            up_pre = dot(rows_in[whole, :], weights[:, shifted], NN)
            sig = jax.nn.sigmoid(gate_pre)
            gate_part = rows_grad * up_pre * sig * (1.0 + gate_pre * (1.0 - sig))
            parts[whole, tile] = gate_part.astype(bf16)
            parts[whole, shifted] = (rows_grad * gate_pre * sig).astype(bf16)

        def back_tile(n, inner):
            source = pl.ds(pl.multiple_of(n * 256, 256), 256)
            rows_back = dot(parts[whole, :], weights[source, :], NT).astype(bf16)
            back[at, :, source] = rows_back[:ROWS, :].reshape(GROUP, 8, 256)
            last_rows[pl.ds(pl.multiple_of(n * GROUP, GROUP), GROUP), :] = rows_back[ROWS:, :]
            return inner

        lax.fori_loop(0, 8, back_tile, 0)
        tails = dot(spread, last_rows[...], NN).astype(bf16)
        back[at, :, D : D + TAIL] = tails.reshape(GROUP, 8, TAIL)

        def start(step, inner):
            order = first + lax.rem(step + turn, GROUP)
            copy = pltpu.make_async_remote_copy(
                src_ref=back.at[order], dst_ref=back_recv.at[order], send_sem=back_sem,
                recv_sem=back_recv_sem.at[g], device_id=place_of(order, -1, here), device_id_type=MESH,
            )
            pl.when(order > 0)(copy.start)
            return inner

        lax.fori_loop(0, GROUP, start, 0)
        return carry

    lax.fori_loop(0, GROUPS, work, 0)
    pltpu.make_async_copy(back.at[0], back_recv.at[0], back_recv_sem.at[0]).start()

    for dx in (1, 3, 2):
        for copy in head_remote(2 * dx)[1:]:
            copy.wait_recv()
        for copy in hand_on(dx):
            copy.start()

    def weight_grads(f, carry):
        tile = pl.ds(pl.multiple_of(f * 256, 256), 256)
        stage[tile, :] = dot(rows_in[:, tile], parts[...], TN).astype(bf16)
        pltpu.make_async_copy(
            stage.at[tile, pl.ds(0, FFE)], gate_out.at[tile, :], out_sem.at[0]
        ).start()
        pltpu.make_async_copy(
            stage.at[tile, pl.ds(FFE, FFE)], up_out.at[tile, :], out_sem.at[1]
        ).start()
        return carry

    lax.fori_loop(0, 8, weight_grads, 0)

    slot_of = lax.rem(iota((tokens, ROWS), 1), 8)
    total[...] = jnp.zeros_like(total)

    def combine(g, carry):
        at = pl.ds(g * GROUP, GROUP)
        pltpu.make_async_copy(back_recv.at[at], back_recv.at[at], back_recv_sem.at[g]).wait()
        hot_part = hot_t[:, pl.ds(pl.multiple_of(g * ROWS, ROWS), ROWS)]
        last_part = hot_t[:, pl.ds(pl.multiple_of(1024 + g * ROWS, ROWS), ROWS)]
        tails = back_recv[at, :, D : D + TAIL].reshape(ROWS, TAIL)
        for n in range(8):
            tile = slice(n * 256, (n + 1) * 256)
            routed = dot(hot_part, back_recv[at, :, tile].reshape(ROWS, 256), NN)
            chosen = jnp.where(slot_of == n, last_part, jnp.zeros((), bf16))
            total[:, tile] += routed + dot(chosen, tails, NN)
        return carry

    lax.fori_loop(0, GROUPS, combine, 0)
    state = state_ref[...].astype(f32)
    rstd = lax.rsqrt(jnp.mean(state * state, axis=-1, keepdims=True) + 1e-06)
    inner = jnp.zeros((tokens, 1), f32)
    weighted = []
    for n in range(8):
        tile = slice(n * 256, (n + 1) * 256)
        weighted.append(gain[:, tile] * total[:, tile])
        inner += jnp.sum(weighted[n] * (state[:, tile] * rstd), axis=-1, keepdims=True)
    inner = inner * (1.0 / D)
    for n in range(8):
        tile = slice(n * 256, (n + 1) * 256)
        change = rstd * (weighted[n] - state[:, tile] * rstd * inner)
        residual_ref[:, tile] = (layer_ref[:, tile].astype(f32) + change).astype(bf16)

    pltpu.make_async_copy(stage.at[:, pl.ds(0, FFE)], gate_out, out_sem.at[0]).wait()
    pltpu.make_async_copy(stage.at[:, pl.ds(FFE, FFE)], up_out, out_sem.at[1]).wait()
    pltpu.make_async_copy(
        send.at[pl.ds(1, 127)], recv.at[pl.ds(1, 127)], send_sem
    ).wait()
    pltpu.make_async_copy(
        back.at[pl.ds(1, 127)], back_recv.at[pl.ds(1, 127)], back_sem
    ).wait()
    for copy in own:
        copy.wait()

    for step in range(1, 8):
        copies = head_remote(step)
        copies[0].wait()
        if step == 1:
            for copy in copies[1:]:
                copy.wait()
        elif step % 2 == 0:
            for copy in copies[1:]:
                copy.wait_send()
        else:
            for copy in hand_on(step // 2):
                copy.wait()


def expert_block(state, gain, layer_grad, grads, routes, w_gate, w_up, queries, keys, values):
    tokens = state.shape[0]
    bf16, f32 = jnp.bfloat16, jnp.float32
    vmem, hbm = pl.BlockSpec(memory_space=pltpu.VMEM), pl.BlockSpec(memory_space=pl.ANY)
    length = tokens * lax.axis_size("seq")
    dma = pltpu.SemaphoreType.DMA
    return pl.pallas_call(
        expert_kernel,
        out_shape=(
            jax.ShapeDtypeStruct((tokens, D), bf16),
            jax.ShapeDtypeStruct(w_gate.shape, bf16),
            jax.ShapeDtypeStruct(w_up.shape, bf16),
            jax.ShapeDtypeStruct((length, 512), bf16),
            jax.ShapeDtypeStruct((length, HEAD_SIZE), bf16),
            jax.ShapeDtypeStruct((length, HEAD_SIZE), bf16),
        ),
        in_specs=[vmem] * 5 + [hbm] * 5,
        out_specs=(vmem,) + (hbm,) * 5,
        scratch_shapes=[
            pltpu.VMEM((128, 8, MESSAGE), bf16),
            pltpu.VMEM((128, 8, MESSAGE), bf16),
            pltpu.VMEM((128, 8, D + TAIL), bf16),
            pltpu.VMEM((128, 8, D + TAIL), bf16),
            pltpu.VMEM((D, 2 * FFE), bf16),
            pltpu.VMEM((GROUPS * PART, D), bf16),
            pltpu.VMEM((GROUPS * PART, 2 * FFE), bf16),
            pltpu.VMEM((D, 2 * FFE), bf16),
            pltpu.VMEM((tokens, D), bf16),
            pltpu.VMEM((1024, tokens), bf16),
            pltpu.VMEM((tokens, 2048), bf16),
            pltpu.VMEM((128, tokens), bf16),
            pltpu.VMEM((1, tokens * TOP), f32),
            pltpu.VMEM((ROWS, TAIL), bf16),
            pltpu.VMEM((tokens, D), f32),
            dma((2,)),
            dma,
            dma((GROUPS,)),
            dma,
            dma((GROUPS,)),
            dma((2,)),
            dma((3, 8)),
            dma((3, 8)),
        ],
        compiler_params=pltpu.CompilerParams(
            collective_id=1, has_side_effects=True, vmem_limit_bytes=60 << 20
        ),
        cost_estimate=pl.CostEstimate(
            flops=30_000_000_000, bytes_accessed=20_000_000, transcendentals=1_000_000
        ),
        name="expert_block",
    )(state, gain, layer_grad, grads, routes, w_gate, w_up, queries, keys, values)


def finish_kernel(count, *refs):
    sources, targets, sems = refs[:count], refs[count : 2 * count], refs[2 * count]
    copies = [
        pltpu.make_async_copy(sources[n], targets[n], sems.at[n]) for n in range(count)
    ]
    for copy in copies:
        copy.start()
    for copy in copies:
        copy.wait()


def finish(*arrays):
    hbm = pl.BlockSpec(memory_space=pl.ANY)
    return pl.pallas_call(
        functools.partial(finish_kernel, len(arrays)),
        out_shape=tuple(jax.ShapeDtypeStruct(a.shape, a.dtype) for a in arrays),
        in_specs=[hbm] * len(arrays),
        out_specs=(hbm,) * len(arrays),
        scratch_shapes=[pltpu.SemaphoreType.DMA((len(arrays),))],
        compiler_params=pltpu.CompilerParams(vmem_limit_bytes=1 << 20),
        name="finish",
    )(*arrays)


def local(
    queries,
    keys,
    values,
    w_out,
    hidden_state,
    norm_gain,
    layer_grad,
    hidden_grad,
    routes,
    w_gate,
    w_up,
):
    residual_rows, gate_grad, up_grad, query_all, key_all, value_all = expert_block(
        hidden_state[0],
        norm_gain.reshape(D // 128, 128),
        layer_grad[0],
        hidden_grad[0].reshape(-1, FFE),
        routes[0].T,
        w_gate[0],
        w_up[0],
        queries[0],
        keys[0],
        values[0],
    )
    query_out, key_out, value_out = attention_core(
        residual_rows, w_out, query_all, key_all, value_all
    )
    outs = (query_out, key_out, value_out, residual_rows, gate_grad, up_grad)
    return tuple(out[None] for out in finish(*outs))


def solution(mesh):
    return jax.shard_map(
        local,
        mesh=mesh,
        in_specs=(
            P("expert", "seq", None),
            P("expert", "seq", None),
            P("expert", "seq", None),
            P("seq", None),
            P("expert", "seq", None),
            P(),
            P("expert", "seq", None),
            P("expert", "seq", None, None),
            P("expert", "seq", None),
            P(("seq", "expert"), None, None),
            P(("seq", "expert"), None, None),
        ),
        out_specs=(
            P("expert", "seq", None),
            P("expert", "seq", None),
            P("expert", "seq", None),
            P("expert", "seq", None),
            P(("seq", "expert"), None, None),
            P(("seq", "expert"), None, None),
        ),
        check_vma=False,
    )
```

```python
import functools

import jax
import jax.numpy as jnp
from jax import lax
from jax.experimental import pallas as pl
from jax.experimental.pallas import tpu as pltpu
from jax.sharding import PartitionSpec as P

D = 2048
QUERY_HEADS = 32
KEY_VALUE_HEADS = 4
HEAD_SIZE = 128
FFE = 768
TOP = 8
LOG2E = 1.4426950408889634

NN = (((1,), (0,)), ((), ()))
NT = (((1,), (1,)), ((), ()))
TN = (((0,), (0,)), ((), ()))
MESH = pl.DeviceIdType.MESH


def dot(a, b, dims):
    return lax.dot_general(a, b, dims, preferred_element_type=jnp.float32)


def attention_kernel(
    residual_ref, w_hbm, query_hbm, key_hbm, value_hbm, query_out, key_out, value_out,
    gathered, w_out, queries, keys, values, grad, key_t, dk, dv, packed, returned,
    probs_0, probs_1, probs_2, probs_3, load_sem, gather_send, gather_recv,
    query_send, query_recv, pair_send, pair_recv,
):
    seq, expert = lax.axis_index("seq"), lax.axis_index("expert")
    x, c = seq // 2, lax.rem(seq, 2)
    tokens = residual_ref.shape[0]
    half = tokens // 2
    bf16, f32 = jnp.bfloat16, jnp.float32
    factor = HEAD_SIZE ** (-0.5)
    probs = (probs_0, probs_1, probs_2, probs_3)
    block = 2 * tokens

    def device(dx, dc):
        return lax.rem(x + dx, 4) * 2 + lax.rem(c + dc, 2)

    barrier = pltpu.get_barrier_semaphore()
    for step in range(1, 8):
        pl.semaphore_signal(
            barrier, inc=1, device_id=(device(step // 2, step % 2), expert), device_id_type=MESH
        )
    loads = [
        pltpu.make_async_copy(source, target, load_sem.at[n])
        for n, (source, target) in enumerate(
            ((query_hbm, queries), (key_hbm, keys), (value_hbm, values), (w_hbm, w_out))
        )
    ]
    for load in loads:
        load.start()

    def rows_of(owner, start, size):
        return pl.ds(pl.multiple_of(owner * tokens + start, size), size)

    def gather_copy(number, owner, start, size, to):
        rows = rows_of(owner, start, size)
        return pltpu.make_async_remote_copy(
            src_ref=gathered.at[rows, :], dst_ref=gathered.at[rows, :],
            send_sem=gather_send.at[number], recv_sem=gather_recv.at[number],
            device_id=(to, expert), device_id_type=MESH,
        )

    own, left, right, far = device(0, 0), device(3, 0), device(1, 0), device(2, 0)
    mate = device(0, 1)
    gathered[rows_of(own, 0, tokens), :] = residual_ref[...]
    pl.semaphore_wait(barrier, 7)
    copies = [
        gather_copy(0, own, 0, half, right),
        gather_copy(1, own, half, half, left),
        gather_copy(2, own, half, half, right),
        gather_copy(3, own, 0, half, left),
        gather_copy(4, own, 0, tokens, mate),
        gather_copy(5, left, 0, half, right),
        gather_copy(6, right, half, half, left),
        gather_copy(7, left, 0, half, mate),
        gather_copy(8, right, half, half, mate),
        gather_copy(9, left, half, half, mate),
        gather_copy(10, right, 0, half, mate),
        gather_copy(11, far, 0, half, mate),
        gather_copy(12, far, half, half, mate),
    ]
    for copy in copies[:5]:
        copy.start()
    for load in loads:
        load.wait()

    key_t[...] = keys[...].astype(f32).T.astype(bf16)
    dk[...] = jnp.zeros_like(dk)
    dv[...] = jnp.zeros_like(dv)

    def softmax_block(i):
        lower, upper = i * block, (i + 1) * block
        key_pos = lax.broadcasted_iota(jnp.int32, (block, block), 0)
        query_pos = lax.broadcasted_iota(jnp.int32, (block, block), 1)
        for head in range(4):
            columns = slice(head * HEAD_SIZE, (head + 1) * HEAD_SIZE)
            scores = dot(keys[0:upper, :], queries[lower:upper, columns], NT) * (factor * LOG2E)
            diagonal = jnp.where(key_pos <= query_pos, scores[lower:upper], -1e30)
            scores = diagonal if i == 0 else jnp.concatenate([scores[:lower], diagonal], axis=0)
            exps = jnp.exp2(scores - jnp.max(scores, axis=0, keepdims=True))
            probs[i][head, :, :] = exps * (1.0 / jnp.sum(exps, axis=0, keepdims=True))

    def project(owner):
        rows = rows_of(owner, 0, tokens)
        grad[rows, :] = dot(gathered[rows, :], w_out[...], NT).astype(bf16)

    softmax_block(0)
    softmax_block(1)
    copies[0].wait_recv()
    copies[5].start()
    copies[7].start()
    copies[1].wait_recv()
    copies[6].start()
    copies[8].start()
    softmax_block(2)
    copies[2].wait_recv()
    copies[9].start()
    copies[3].wait_recv()
    copies[10].start()
    softmax_block(3)
    project(own)
    copies[4].wait_recv()
    project(mate)
    project(left)
    project(right)
    copies[5].wait_recv()
    copies[11].start()
    copies[6].wait_recv()
    copies[12].start()
    project(far)
    for copy in copies[7:11]:
        copy.wait_recv()
    project(device(3, 1))
    project(device(1, 1))
    for copy in copies[11:]:
        copy.wait_recv()
    project(device(2, 1))

    def backward_block(i, part):
        lower, upper = i * block, (i + 1) * block
        for head in (2 * part, 2 * part + 1):
            columns = slice(head * HEAD_SIZE, (head + 1) * HEAD_SIZE)
            out_grad = grad[lower:upper, columns]
            prob = probs[i][head]
            dv[0:upper, :] += dot(prob.astype(bf16), out_grad, NN)
            prob_grad = dot(values[0:upper, :], out_grad, NT)
            delta = jnp.sum(prob * prob_grad, axis=0, keepdims=True)
            score_grad = (prob * (prob_grad - delta)).astype(bf16)
            dk[0:upper, :] += dot(score_grad, queries[lower:upper, columns], NN)
            query_grad = dot(key_t[:, 0:upper], score_grad, NN) * factor
            packed[lower:upper, columns] = query_grad.T.astype(bf16)

    pair = slice(4 * HEAD_SIZE, 6 * HEAD_SIZE)

    def own_columns(part):
        return pl.ds(pl.multiple_of(seq * 512 + part * 256, 256), 256)

    def query_copy(dx, dc, part):
        to, number = device(dx, dc), part * 8 + dx * 2 + dc
        return pltpu.make_async_remote_copy(
            src_ref=packed.at[rows_of(to, 0, tokens), pl.ds(part * 256, 256)],
            dst_ref=query_out.at[:, own_columns(part)],
            send_sem=query_send.at[number], recv_sem=query_recv.at[number],
            device_id=(to, expert), device_id_type=MESH,
        )

    def pair_copy(dx, dc):
        to, number = device(dx, dc), dx * 2 + dc
        return pltpu.make_async_remote_copy(
            src_ref=packed.at[rows_of(to, 0, tokens), pl.ds(512, 256)],
            dst_ref=returned.at[seq],
            send_sem=pair_send.at[number], recv_sem=pair_recv.at[number],
            device_id=(to, expert), device_id_type=MESH,
        )

    own_query = [
        pltpu.make_async_copy(
            packed.at[rows_of(seq, 0, tokens), pl.ds(part * 256, 256)],
            query_out.at[:, own_columns(part)],
            query_send.at[part * 8],
        )
        for part in range(2)
    ]

    def backward_step(step, carry):
        dx = lax.rem(step + 1, 4)
        chip = lax.rem(x + dx, 4)
        for part in range(2):
            for i in range(4):
                pl.when(chip == i)(functools.partial(backward_block, i, part))
            pl.when(step < 3)(query_copy(dx, 0, part).start)
            pl.when(step == 3)(own_query[part].start)
            query_copy(dx, 1, part).start()
        return carry

    lax.fori_loop(0, 4, backward_step, 0)
    packed[:, 512:640] = (dk[...] * factor).astype(bf16)
    packed[:, 640:768] = dv[...].astype(bf16)
    for step in (2, 3, 4, 5, 6, 7, 1):
        pair_copy(step // 2, step % 2).start()
    returned[seq, :, :] = packed[rows_of(seq, 0, tokens), pair]
    for step in range(1, 8):
        pair_copy(step // 2, step % 2).wait_recv()
    for head in range(KEY_VALUE_HEADS):
        total = returned[2 * head].astype(f32) + returned[2 * head + 1].astype(f32)
        columns = slice(head * HEAD_SIZE, (head + 1) * HEAD_SIZE)
        key_out[:, columns] = total[:, 0:HEAD_SIZE].astype(bf16)
        value_out[:, columns] = total[:, HEAD_SIZE:].astype(bf16)
    for copy in copies:
        copy.wait_send()
    for step in range(1, 8):
        for part in range(2):
            query_copy(step // 2, step % 2, part).wait()
        pair_copy(step // 2, step % 2).wait_send()
    for copy in own_query:
        copy.wait()


def attention_core(residual, w_out, queries, keys, values):
    tokens, length = residual.shape[0], queries.shape[0]
    bf16, f32 = jnp.bfloat16, jnp.float32
    vmem, hbm = pl.BlockSpec(memory_space=pltpu.VMEM), pl.BlockSpec(memory_space=pl.ANY)
    dma = pltpu.SemaphoreType.DMA
    return pl.pallas_call(
        attention_kernel,
        out_shape=(
            jax.ShapeDtypeStruct((tokens, QUERY_HEADS * HEAD_SIZE), bf16),
            jax.ShapeDtypeStruct((tokens, KEY_VALUE_HEADS * HEAD_SIZE), bf16),
            jax.ShapeDtypeStruct((tokens, KEY_VALUE_HEADS * HEAD_SIZE), bf16),
        ),
        in_specs=[vmem] + [hbm] * 4,
        out_specs=(hbm, vmem, vmem),
        scratch_shapes=[
            pltpu.VMEM((length, D), bf16),
            pltpu.VMEM(w_out.shape, bf16),
            pltpu.VMEM(queries.shape, bf16),
            pltpu.VMEM(keys.shape, bf16),
            pltpu.VMEM(values.shape, bf16),
            pltpu.VMEM((length, 512), bf16),
            pltpu.VMEM((HEAD_SIZE, length), bf16),
            pltpu.VMEM((length, HEAD_SIZE), f32),
            pltpu.VMEM((length, HEAD_SIZE), f32),
            pltpu.VMEM((length, 768), bf16),
            pltpu.VMEM((8, tokens, 256), bf16),
            pltpu.VMEM((4, 256, 256), f32),
            pltpu.VMEM((4, 512, 256), f32),
            pltpu.VMEM((4, 768, 256), f32),
            pltpu.VMEM((4, 1024, 256), f32),
            dma((4,)),
            dma((13,)),
            dma((13,)),
            dma((16,)),
            dma((16,)),
            dma((8,)),
            dma((8,)),
        ],
        compiler_params=pltpu.CompilerParams(
            collective_id=2, has_side_effects=True, vmem_limit_bytes=56 << 20
        ),
        cost_estimate=pl.CostEstimate(
            flops=9_000_000_000, bytes_accessed=10_000_000, transcendentals=3_000_000
        ),
        name="attention_core",
    )(residual, w_out, queries, keys, values)


ORDER = 101
GROUP = 32
GROUPS = 4
ROWS = GROUP * 8
PART = ROWS + GROUP
TAIL = D // 8
WIDE = D + FFE
MESSAGE = WIDE + TAIL + HEAD_SIZE


def place_of(order, sign, here):
    x, c, y, z = here
    code = lax.rem(order * ORDER, 128)
    dc, dx, dy, dz = lax.rem(code, 2), lax.rem(code // 2, 4), lax.rem(code // 8, 4), code // 32
    if sign < 0:
        dx, dy, dz = 4 - dx, 4 - dy, 4 - dz
    return (
        lax.rem(x + dx, 4) * 2 + lax.rem(c + dc, 2),
        lax.rem(y + dy, 4) * 4 + lax.rem(z + dz, 4),
    )


def expert_of(order, here):
    seq, expert = place_of(order, 1, here)
    return seq * 16 + expert


def expert_kernel(
    state_ref, gain_ref, layer_ref, grads_ref, routes_ref, gate_hbm, up_hbm, query_hbm, key_hbm,
    value_hbm, residual_ref, gate_out, up_out, query_all, key_all, value_all,
    send, recv, back, back_recv, weights, rows_in, parts, stage, expert_in, hot, hot_t, last,
    codes, last_rows, total, weight_sem, send_sem, recv_sem, back_sem, back_recv_sem, out_sem,
    head_send, head_recv,
):
    seq, expert = lax.axis_index("seq"), lax.axis_index("expert")
    here = (seq // 2, lax.rem(seq, 2), expert // 4, lax.rem(expert, 4))
    turn = seq * 4 + expert * 2 + expert // 4
    tokens = state_ref.shape[0]
    bf16, f32 = jnp.bfloat16, jnp.float32

    def iota(shape, axis):
        return lax.broadcasted_iota(jnp.int32, shape, axis)

    barrier = pltpu.get_barrier_semaphore()

    def greet(order, carry):
        pl.semaphore_signal(barrier, inc=1, device_id=place_of(order, 1, here), device_id_type=MESH)
        return carry

    lax.fori_loop(1, 128, greet, 0)
    gate_copy = pltpu.make_async_copy(gate_hbm, weights.at[:, pl.ds(0, FFE)], weight_sem.at[0])
    up_copy = pltpu.make_async_copy(up_hbm, weights.at[:, pl.ds(FFE, FFE)], weight_sem.at[1])
    gate_copy.start()
    up_copy.start()

    gain = gain_ref[...].astype(f32)
    gain = jnp.concatenate([gain[j : j + 1, :] for j in range(D // 128)], axis=1)
    state = state_ref[...].astype(f32)
    rstd = lax.rsqrt(jnp.mean(state * state, axis=-1, keepdims=True) + 1e-06)
    expert_in[...] = (state * rstd * gain).astype(bf16)

    pl.semaphore_wait(barrier, 127)

    def head_copies(step):
        dx, dc = step // 2, lax.rem(step, 2)
        to = lax.rem(here[0] + dx, 4) * 2 + lax.rem(here[1] + dc, 2)
        rows = pl.ds(pl.multiple_of(seq * tokens, tokens), tokens)
        wide = pl.ds(pl.multiple_of(to * 512, 512), 512)
        narrow = pl.ds(pl.multiple_of(to // 2 * HEAD_SIZE, HEAD_SIZE), HEAD_SIZE)
        return to, (
            (query_hbm.at[:, wide], query_all.at[rows, :]),
            (key_hbm.at[:, narrow], key_all.at[rows, :]),
            (value_hbm.at[:, narrow], value_all.at[rows, :]),
        )

    def head_remote(step):
        to, pairs = head_copies(step)
        return [
            pltpu.make_async_remote_copy(
                src_ref=source, dst_ref=target_ref, send_sem=head_send.at[n, step],
                recv_sem=head_recv.at[n, step], device_id=(to, expert), device_id_type=MESH,
            )
            for n, (source, target_ref) in enumerate(pairs)
        ]

    own = [
        pltpu.make_async_copy(source, target_ref, head_send.at[n, 0])
        for n, (source, target_ref) in enumerate(head_copies(0)[1])
    ]
    for copy in own:
        copy.start()

    for step in (2, 6, 4, 1, 3, 5, 7):
        copies = head_remote(step)
        for copy in copies if step in (1, 2, 4, 6) else copies[:1]:
            copy.start()

    def hand_on(dx):
        rows = pl.ds(
            pl.multiple_of((lax.rem(here[0] + 4 - dx, 4) * 2 + here[1]) * tokens, tokens), tokens
        )
        mate = here[0] * 2 + 1 - here[1]
        return [
            pltpu.make_async_remote_copy(
                src_ref=array.at[rows, :], dst_ref=array.at[rows, :],
                send_sem=head_send.at[n, 2 * dx + 1], recv_sem=head_recv.at[n, 2 * dx + 1],
                device_id=(mate, expert), device_id_type=MESH,
            )
            for n, array in ((1, key_all), (2, value_all))
        ]


    lanes = iota((tokens, 128), 1)
    route = routes_ref[...].astype(f32).T
    named = [route[:, k : k + 1] == lanes.astype(f32) for k in range(TOP)]
    count = sum(jnp.where(n, 1.0, 0.0) for n in named)
    earlier = jnp.where(iota((tokens, tokens), 0) > iota((tokens, tokens), 1), 1.0, 0.0)
    rank = dot(earlier.astype(bf16), count.astype(bf16), NN)
    columns = iota((tokens, tokens * TOP), 1) - iota((tokens, tokens * TOP), 0) * TOP
    spread_codes = jnp.zeros((tokens, tokens * TOP), f32)
    for k in range(TOP):
        route_rank = jnp.sum(jnp.where(named[k], rank, 0.0), axis=1, keepdims=True)
        code = route[:, k : k + 1] * 16.0 + route_rank
        spread_codes = jnp.where(columns == k, code, spread_codes)
    codes[...] = jnp.sum(spread_codes, axis=0, keepdims=True)
    target = expert_of(iota((128, 128), 0), here)
    ordered = jnp.where(target == iota((128, 128), 1), 1.0, 0.0).astype(bf16)
    rank_t = dot(ordered, jnp.where(count > 0.0, rank, -1.0).astype(bf16), NT)
    slot = iota((128, 8, tokens), 1).astype(f32)
    rank_wide = jnp.broadcast_to(rank_t[:, None, :], (128, 8, tokens))
    hot_full = jnp.where(rank_wide == slot, 1.0, 0.0).reshape(1024, tokens)
    hot[...] = hot_full.astype(bf16)
    hot_t[:, 0:1024] = hot_full.T.astype(bf16)
    last_full = jnp.where(rank_wide == 8.0, 1.0, 0.0).reshape(1024, tokens)
    hot_t[:, 1024:2048] = last_full.T.astype(bf16)
    last[...] = jnp.where(rank_t == 8.0, 1.0, 0.0).astype(bf16)

    row, col = iota((ROWS, ROWS), 0), iota((ROWS, ROWS), 1)
    spread = jnp.where(col == lax.rem(row, 8) * GROUP + row // 8, 1.0, 0.0).astype(bf16)
    gather = jnp.where(row == lax.rem(col, 8) * GROUP + col // 8, 1.0, 0.0).astype(bf16)

    def dispatch(g, carry):
        at = pl.ds(g * GROUP, GROUP)
        rows = pl.ds(pl.multiple_of(g * ROWS, ROWS), ROWS)
        first = g * GROUP
        x_rows = dot(hot[rows, :], expert_in[...], NN).astype(bf16)
        send[at, :, 0:D] = x_rows.reshape(GROUP, 8, D)
        number = iota((ROWS, 128), 0)
        row_code = (expert_of(first + number // 8, here) * 16 + lax.rem(number, 8)).astype(f32)
        last_code = (expert_of(first + iota((GROUP, 128), 0), here) * 16 + 8).astype(f32)

        def one_hot(code):
            pieces = [
                jnp.where(codes[:, j * 128 : (j + 1) * 128] == code, 1.0, 0.0).astype(bf16)
                for j in range(TOP)
            ]
            return jnp.concatenate(pieces, axis=1)

        h_rows = dot(one_hot(row_code), grads_ref[...], NN).astype(bf16)
        send[at, :, D:WIDE] = h_rows.reshape(GROUP, 8, FFE)
        x_last = dot(last[pl.ds(pl.multiple_of(first, GROUP), GROUP), :], expert_in[...], NN)
        x_last = x_last.astype(bf16)
        h_last = dot(one_hot(last_code), grads_ref[...], NN).astype(bf16)
        x_stack = jnp.concatenate([x_last[:, s * TAIL : (s + 1) * TAIL] for s in range(8)], axis=0)
        h_stack = jnp.concatenate([h_last[:, s * 128 : (s + 1) * 128] for s in range(6)], axis=0)
        x_tail = dot(spread, x_stack, NN).astype(bf16)
        h_tail = dot(spread[:, 0 : 6 * GROUP], h_stack, NN).astype(bf16)
        send[at, :, WIDE : WIDE + TAIL] = x_tail.reshape(GROUP, 8, TAIL)
        send[at, :, WIDE + TAIL : MESSAGE] = h_tail.reshape(GROUP, 8, HEAD_SIZE)

        def start(step, inner):
            order = first + lax.rem(step + turn, GROUP)
            copy = pltpu.make_async_remote_copy(
                src_ref=send.at[order], dst_ref=recv.at[order], send_sem=send_sem,
                recv_sem=recv_sem.at[g], device_id=place_of(order, 1, here), device_id_type=MESH,
            )
            pl.when(order > 0)(copy.start)
            return inner

        lax.fori_loop(0, GROUP, start, 0)
        return carry

    lax.fori_loop(0, GROUPS, dispatch, 0)
    pltpu.make_async_copy(send.at[0], recv.at[0], recv_sem.at[0]).start()
    gate_copy.wait()
    up_copy.wait()

    def work(g, carry):
        at = pl.ds(g * GROUP, GROUP)
        first = g * GROUP
        whole = pl.ds(pl.multiple_of(g * PART, GROUP), PART)
        main = pl.ds(pl.multiple_of(g * PART, GROUP), ROWS)
        tail = pl.ds(pl.multiple_of(g * PART + ROWS, GROUP), GROUP)
        pltpu.make_async_copy(recv.at[at], recv.at[at], recv_sem.at[g]).wait()
        rows_in[main, :] = recv[at, :, 0:D].reshape(ROWS, D)
        x_last = dot(gather, recv[at, :, WIDE : WIDE + TAIL].reshape(ROWS, TAIL), NN).astype(bf16)
        for s in range(8):
            rows_in[tail, s * TAIL : (s + 1) * TAIL] = x_last[s * GROUP : (s + 1) * GROUP, :]
        h_last = dot(
            gather, recv[at, :, WIDE + TAIL : MESSAGE].reshape(ROWS, HEAD_SIZE), NN
        )
        h_last = jnp.concatenate([h_last[s * GROUP : (s + 1) * GROUP, :] for s in range(6)], axis=1)
        for n in range(3):
            tile = slice(n * 256, (n + 1) * 256)
            shifted = slice(FFE + n * 256, FFE + (n + 1) * 256)
            rows_grad = jnp.concatenate(
                [
                    recv[at, :, D + n * 256 : D + (n + 1) * 256].reshape(ROWS, 256).astype(f32),
                    h_last[:, tile],
                ],
                axis=0,
            )
            gate_pre = dot(rows_in[whole, :], weights[:, tile], NN)
            up_pre = dot(rows_in[whole, :], weights[:, shifted], NN)
            sig = jax.nn.sigmoid(gate_pre)
            gate_part = rows_grad * up_pre * sig * (1.0 + gate_pre * (1.0 - sig))
            parts[whole, tile] = gate_part.astype(bf16)
            parts[whole, shifted] = (rows_grad * gate_pre * sig).astype(bf16)

        def back_tile(n, inner):
            source = pl.ds(pl.multiple_of(n * 256, 256), 256)
            rows_back = dot(parts[whole, :], weights[source, :], NT).astype(bf16)
            back[at, :, source] = rows_back[:ROWS, :].reshape(GROUP, 8, 256)
            last_rows[pl.ds(pl.multiple_of(n * GROUP, GROUP), GROUP), :] = rows_back[ROWS:, :]
            return inner

        lax.fori_loop(0, 8, back_tile, 0)
        tails = dot(spread, last_rows[...], NN).astype(bf16)
        back[at, :, D : D + TAIL] = tails.reshape(GROUP, 8, TAIL)

        def start(step, inner):
            order = first + lax.rem(step + turn, GROUP)
            copy = pltpu.make_async_remote_copy(
                src_ref=back.at[order], dst_ref=back_recv.at[order], send_sem=back_sem,
                recv_sem=back_recv_sem.at[g], device_id=place_of(order, -1, here), device_id_type=MESH,
            )
            pl.when(order > 0)(copy.start)
            return inner

        lax.fori_loop(0, GROUP, start, 0)
        return carry

    lax.fori_loop(0, GROUPS, work, 0)
    pltpu.make_async_copy(back.at[0], back_recv.at[0], back_recv_sem.at[0]).start()

    for dx in (1, 3, 2):
        for copy in head_remote(2 * dx)[1:]:
            copy.wait_recv()
        for copy in hand_on(dx):
            copy.start()

    def weight_grads(f, carry):
        tile = pl.ds(pl.multiple_of(f * 256, 256), 256)
        stage[tile, :] = dot(rows_in[:, tile], parts[...], TN).astype(bf16)
        pltpu.make_async_copy(
            stage.at[tile, pl.ds(0, FFE)], gate_out.at[tile, :], out_sem.at[0]
        ).start()
        pltpu.make_async_copy(
            stage.at[tile, pl.ds(FFE, FFE)], up_out.at[tile, :], out_sem.at[1]
        ).start()
        return carry

    lax.fori_loop(0, 8, weight_grads, 0)

    slot_of = lax.rem(iota((tokens, ROWS), 1), 8)
    total[...] = jnp.zeros_like(total)

    def combine(g, carry):
        at = pl.ds(g * GROUP, GROUP)
        pltpu.make_async_copy(back_recv.at[at], back_recv.at[at], back_recv_sem.at[g]).wait()
        hot_part = hot_t[:, pl.ds(pl.multiple_of(g * ROWS, ROWS), ROWS)]
        last_part = hot_t[:, pl.ds(pl.multiple_of(1024 + g * ROWS, ROWS), ROWS)]
        tails = back_recv[at, :, D : D + TAIL].reshape(ROWS, TAIL)
        for n in range(8):
            tile = slice(n * 256, (n + 1) * 256)
            routed = dot(hot_part, back_recv[at, :, tile].reshape(ROWS, 256), NN)
            chosen = jnp.where(slot_of == n, last_part, jnp.zeros((), bf16))
            total[:, tile] += routed + dot(chosen, tails, NN)
        return carry

    lax.fori_loop(0, GROUPS, combine, 0)
    state = state_ref[...].astype(f32)
    rstd = lax.rsqrt(jnp.mean(state * state, axis=-1, keepdims=True) + 1e-06)
    inner = jnp.zeros((tokens, 1), f32)
    weighted = []
    for n in range(8):
        tile = slice(n * 256, (n + 1) * 256)
        weighted.append(gain[:, tile] * total[:, tile])
        inner += jnp.sum(weighted[n] * (state[:, tile] * rstd), axis=-1, keepdims=True)
    inner = inner * (1.0 / D)
    for n in range(8):
        tile = slice(n * 256, (n + 1) * 256)
        change = rstd * (weighted[n] - state[:, tile] * rstd * inner)
        residual_ref[:, tile] = (layer_ref[:, tile].astype(f32) + change).astype(bf16)

    pltpu.make_async_copy(stage.at[:, pl.ds(0, FFE)], gate_out, out_sem.at[0]).wait()
    pltpu.make_async_copy(stage.at[:, pl.ds(FFE, FFE)], up_out, out_sem.at[1]).wait()
    pltpu.make_async_copy(
        send.at[pl.ds(1, 127)], recv.at[pl.ds(1, 127)], send_sem
    ).wait()
    pltpu.make_async_copy(
        back.at[pl.ds(1, 127)], back_recv.at[pl.ds(1, 127)], back_sem
    ).wait()
    for copy in own:
        copy.wait()

    for step in range(1, 8):
        copies = head_remote(step)
        copies[0].wait()
        if step == 1:
            for copy in copies[1:]:
                copy.wait()
        elif step % 2 == 0:
            for copy in copies[1:]:
                copy.wait_send()
        else:
            for copy in hand_on(step // 2):
                copy.wait()


def expert_block(state, gain, layer_grad, grads, routes, w_gate, w_up, queries, keys, values):
    tokens = state.shape[0]
    bf16, f32 = jnp.bfloat16, jnp.float32
    vmem, hbm = pl.BlockSpec(memory_space=pltpu.VMEM), pl.BlockSpec(memory_space=pl.ANY)
    length = tokens * lax.axis_size("seq")
    dma = pltpu.SemaphoreType.DMA
    return pl.pallas_call(
        expert_kernel,
        out_shape=(
            jax.ShapeDtypeStruct((tokens, D), bf16),
            jax.ShapeDtypeStruct(w_gate.shape, bf16),
            jax.ShapeDtypeStruct(w_up.shape, bf16),
            jax.ShapeDtypeStruct((length, 512), bf16),
            jax.ShapeDtypeStruct((length, HEAD_SIZE), bf16),
            jax.ShapeDtypeStruct((length, HEAD_SIZE), bf16),
        ),
        in_specs=[vmem] * 5 + [hbm] * 5,
        out_specs=(vmem,) + (hbm,) * 5,
        scratch_shapes=[
            pltpu.VMEM((128, 8, MESSAGE), bf16),
            pltpu.VMEM((128, 8, MESSAGE), bf16),
            pltpu.VMEM((128, 8, D + TAIL), bf16),
            pltpu.VMEM((128, 8, D + TAIL), bf16),
            pltpu.VMEM((D, 2 * FFE), bf16),
            pltpu.VMEM((GROUPS * PART, D), bf16),
            pltpu.VMEM((GROUPS * PART, 2 * FFE), bf16),
            pltpu.VMEM((D, 2 * FFE), bf16),
            pltpu.VMEM((tokens, D), bf16),
            pltpu.VMEM((1024, tokens), bf16),
            pltpu.VMEM((tokens, 2048), bf16),
            pltpu.VMEM((128, tokens), bf16),
            pltpu.VMEM((1, tokens * TOP), f32),
            pltpu.VMEM((ROWS, TAIL), bf16),
            pltpu.VMEM((tokens, D), f32),
            dma((2,)),
            dma,
            dma((GROUPS,)),
            dma,
            dma((GROUPS,)),
            dma((2,)),
            dma((3, 8)),
            dma((3, 8)),
        ],
        compiler_params=pltpu.CompilerParams(
            collective_id=1, has_side_effects=True, vmem_limit_bytes=60 << 20
        ),
        cost_estimate=pl.CostEstimate(
            flops=30_000_000_000, bytes_accessed=20_000_000, transcendentals=1_000_000
        ),
        name="expert_block",
    )(state, gain, layer_grad, grads, routes, w_gate, w_up, queries, keys, values)


def finish_kernel(count, *refs):
    sources, targets, sems = refs[:count], refs[count : 2 * count], refs[2 * count]
    copies = [
        pltpu.make_async_copy(sources[n], targets[n], sems.at[n]) for n in range(count)
    ]
    for copy in copies:
        copy.start()
    for copy in copies:
        copy.wait()


def finish(*arrays):
    hbm = pl.BlockSpec(memory_space=pl.ANY)
    return pl.pallas_call(
        functools.partial(finish_kernel, len(arrays)),
        out_shape=tuple(jax.ShapeDtypeStruct(a.shape, a.dtype) for a in arrays),
        in_specs=[hbm] * len(arrays),
        out_specs=(hbm,) * len(arrays),
        scratch_shapes=[pltpu.SemaphoreType.DMA((len(arrays),))],
        compiler_params=pltpu.CompilerParams(vmem_limit_bytes=1 << 20),
        name="finish",
    )(*arrays)


def local(
    queries,
    keys,
    values,
    w_out,
    hidden_state,
    norm_gain,
    layer_grad,
    hidden_grad,
    routes,
    w_gate,
    w_up,
):
    residual_rows, gate_grad, up_grad, query_all, key_all, value_all = expert_block(
        hidden_state[0],
        norm_gain.reshape(D // 128, 128),
        layer_grad[0],
        hidden_grad[0].reshape(-1, FFE),
        routes[0].T,
        w_gate[0],
        w_up[0],
        queries[0],
        keys[0],
        values[0],
    )
    query_out, key_out, value_out = attention_core(
        residual_rows, w_out, query_all, key_all, value_all
    )
    outs = (query_out, key_out, value_out, residual_rows, gate_grad, up_grad)
    return tuple(out[None] for out in finish(*outs))


def solution(mesh):
    return jax.shard_map(
        local,
        mesh=mesh,
        in_specs=(
            P("expert", "seq", None),
            P("expert", "seq", None),
            P("expert", "seq", None),
            P("seq", None),
            P("expert", "seq", None),
            P(),
            P("expert", "seq", None),
            P("expert", "seq", None, None),
            P("expert", "seq", None),
            P(("seq", "expert"), None, None),
            P(("seq", "expert"), None, None),
        ),
        out_specs=(
            P("expert", "seq", None),
            P("expert", "seq", None),
            P("expert", "seq", None),
            P("expert", "seq", None),
            P(("seq", "expert"), None, None),
            P(("seq", "expert"), None, None),
        ),
        check_vma=False,
    )
```
